256 devices in a mesh: space: 16 (over y, z_lo, core), rot: 16 (over z_hi, x).
Axes of the slice: x: 4, y: 4, z: 8 (z_hi: 4, z_lo: 2; z = z_hi * 2 + z_lo), core: 2. Of those that a mesh axis runs over, the one named last changes fastest.
Arguments:
- tomogram: float32 [256, 6144], P('space'), may hold values from -6 to 6
- templates: bfloat16 [64, 32768], P('space'), may hold values from -6 to 6
- rot_ids: int32 [16], P('rot'), may hold values from 0 to 63
Outputs:
- best_score: float32 [256, 6144], P('space', 'rot')
- score_mass: float32 [256, 6144], P('space', 'rot')
The draws below stay inside these ranges and needn't reach their ends.
Inputs may be any that keep to these rules, and one draw needn't show every extreme that they name: `rot_ids`: each entry names a template of the bank.
All inputs are finite; a program needn't handle non-finite values.
Results may differ from the reference program's by a relative error of at most 0.0003.
Values may be sent and summed in bfloat16 or wider, within the bound.
No kernel may reach another device: no remote copies, remote signals or barrier semaphores. Data moves between devices by JAX's collectives and lax.ppermute only.
A program may use at most 64 MiB of HBM per device.

```python
import jax
import jax.numpy as jnp
from jax import lax

NY = 64
NZ = 96
TS = 32
NX = 256
ROTS = 16
BANK = 64


def set_ends(drawn, key, smallest, largest):
    place = [jax.random.randint(jax.random.fold_in(key, axis), (), 0, length) for axis, length in enumerate(drawn.shape)]
    longest = drawn.shape.index(max(drawn.shape))
    neighbour = place[:longest] + [(place[longest] + 1) % drawn.shape[longest]] + place[longest + 1:]
    return drawn.at[tuple(place)].set(smallest).at[tuple(neighbour)].set(largest)


def levels(rng, extent, shards, low, top_value):
    def one(dim, blocks):
        heights = jax.random.uniform(jax.random.fold_in(jax.random.fold_in(rng, 6), dim), (blocks,), jnp.float32, low / len(shards), top_value / len(shards))
        return jnp.repeat(jnp.exp(heights), extent[dim] // blocks).reshape((-1,) + (1,) * (len(extent) - dim - 1))

    level = one(*shards[0])
    for cut in shards[1:]:
        level = level * one(*cut)
    return level


def gaussian(own_key, dims, width, most, split=(), dtype=jnp.bfloat16):
    factor_of = levels(own_key, dims, split, -0.22, 0.18) if split else 1.0
    entries = jax.random.normal(own_key, dims, jnp.float32) * width * factor_of
    return jnp.minimum(jnp.maximum(entries, -most), most).astype(dtype)


def setup_inputs(seed: int = 0) -> dict:
    streams_of = jax.random.split(jax.random.key(seed), 4)
    tomogram = gaussian(streams_of[0], (NX, NY * NZ), 1.0, 6.0, ((0, 16),), jnp.float32)
    templates = gaussian(streams_of[1], (BANK, TS * TS * TS), 1.0, 6.0, ((0, 16),))
    rot_ids = set_ends(jax.random.randint(streams_of[2], (ROTS,), 0, BANK), jax.random.fold_in(streams_of[2], 1), 0, BANK - 1).astype(jnp.int32)
    return {"tomogram": tomogram, "templates": templates, "rot_ids": rot_ids}


sharpness = 0.4

def band_matrix(length, out_count, window_width):
    row_index = lax.broadcasted_iota(jnp.int32, (length, out_count), 0)
    col_index = lax.broadcasted_iota(jnp.int32, (length, out_count), 1)
    offset = row_index - col_index
    return ((offset >= 0) & (offset < window_width)).astype(jnp.float32)

def box_sum(squares, counts):
    band_x = band_matrix(squares.shape[0], counts[0], TS)
    band_y = band_matrix(squares.shape[1], counts[1], TS)
    band_z = band_matrix(squares.shape[2], counts[2], TS)
    summed = jnp.einsum('abc,av->vbc', squares, band_x, precision=lax.Precision.HIGHEST)
    summed = jnp.einsum('vbc,bw->vwc', summed, band_y, precision=lax.Precision.HIGHEST)
    return jnp.einsum('vwc,cu->vwu', summed, band_z, precision=lax.Precision.HIGHEST)

def standardize(template):
    values = template.astype(jnp.float32)
    centred = values - jnp.mean(values)
    return centred / jnp.sqrt(jnp.mean(centred * centred) + 1e-06)

def reference(tomogram, templates, rot_ids):
    half_width = TS // 2
    volume = tomogram.reshape(NX, NY, NZ)
    padded = jnp.pad(volume, half_width)
    padded_shape = padded.shape
    spectrum = jnp.fft.fftn(padded)
    window = box_sum(padded * padded, (NX, NY, NZ))
    inverse_norm = 1.0 / jnp.sqrt(window + TS ** 3 * 1e-06)

    def accumulate(state_pair, wanted):
        best_now, exp_total = state_pair
        picked = lax.dynamic_index_in_dim(templates, wanted, 0, keepdims=False).reshape(TS, TS, TS)
        normed = standardize(picked)
        placed = jnp.pad(normed, ((0, padded_shape[0] - TS), (0, padded_shape[1] - TS), (0, padded_shape[2] - TS)))
        correlation = jnp.real(jnp.fft.ifftn(spectrum * jnp.conj(jnp.fft.fftn(placed))))[:NX, :NY, :NZ]
        scores = correlation * inverse_norm
        return ((jnp.maximum(best_now, scores), exp_total + jnp.exp(sharpness * scores)), None)
    start_state = (jnp.full((NX, NY, NZ), -jnp.inf, jnp.float32), jnp.zeros((NX, NY, NZ), jnp.float32))
    (best_now, exp_total), ignored = lax.scan(accumulate, start_state, rot_ids)
    return (best_now.reshape(NX, NY * NZ), (jnp.log(exp_total) / sharpness).reshape(NX, NY * NZ))
```

```python
import math

import jax
import jax.numpy as jnp
from jax import lax
from jax.sharding import PartitionSpec as P

NY = 64
NZ = 96
TS = 32
HALF = TS // 2
LX = 48
LY = NY + HALF
LZ = NZ + HALF
KZ = LZ // 2 + 1

sharpness = 0.4


def contract(form, left, right):
    return jnp.einsum(form, left, right, precision=lax.Precision.HIGH)


def dft_tables(length, first, count, out_count):
    row_index = lax.broadcasted_iota(jnp.int32, (count, out_count), 0) + first
    col_index = lax.broadcasted_iota(jnp.int32, (count, out_count), 1)
    phase_index = row_index * col_index % length
    angles = phase_index.astype(jnp.float32) * (2.0 * math.pi / length)
    return (jnp.cos(angles), jnp.sin(angles))


def band_matrix(count):
    row_index = lax.broadcasted_iota(jnp.int32, (count, count), 0) + HALF
    col_index = lax.broadcasted_iota(jnp.int32, (count, count), 1)
    offset = row_index - col_index
    return ((offset >= 0) & (offset < TS)).astype(jnp.float32)


def sliding(planes, count):
    width = 1
    while width < TS:
        planes = planes[: planes.shape[0] - width] + planes[width:]
        width *= 2
    return planes[:count]


def box_sum(squares, count_x):
    summed = sliding(squares, count_x)
    summed = contract("vbc,bw->vwc", summed, band_matrix(NY))
    return contract("vwc,cu->vwu", summed, band_matrix(NZ))


def standardize(template):
    values = template.astype(jnp.float32)
    centred = values - jnp.mean(values)
    return centred / jnp.sqrt(jnp.mean(centred * centred) + 1e-06)


def forward(field, first):
    count_x, count_y, count_z = field.shape
    cos_z, sin_z = dft_tables(LZ, first, count_z, KZ)
    real_z = contract("abn,nk->abk", field, cos_z)
    imag_z = -contract("abn,nk->abk", field, sin_z)
    cos_y, sin_y = dft_tables(LY, first, count_y, LY)
    real_y = contract("ank,nm->amk", real_z, cos_y) + contract("ank,nm->amk", imag_z, sin_y)
    imag_y = contract("ank,nm->amk", imag_z, cos_y) - contract("ank,nm->amk", real_z, sin_y)
    cos_x, sin_x = dft_tables(LX, 0, count_x, LX)
    real_x = contract("nmk,nq->qmk", real_y, cos_x) + contract("nmk,nq->qmk", imag_y, sin_x)
    imag_x = contract("nmk,nq->qmk", imag_y, cos_x) - contract("nmk,nq->qmk", real_y, sin_x)
    return (real_x, imag_x)


def inverse(spec_real, spec_imag, count_x):
    cos_x, sin_x = dft_tables(LX, 0, LX, count_x)
    real_x = contract("kyz,kv->vyz", spec_real, cos_x) - contract("kyz,kv->vyz", spec_imag, sin_x)
    imag_x = contract("kyz,kv->vyz", spec_real, sin_x) + contract("kyz,kv->vyz", spec_imag, cos_x)
    cos_y, sin_y = dft_tables(LY, 0, LY, NY)
    real_y = contract("vkz,kw->vwz", real_x, cos_y) - contract("vkz,kw->vwz", imag_x, sin_y)
    imag_y = contract("vkz,kw->vwz", real_x, sin_y) + contract("vkz,kw->vwz", imag_x, cos_y)
    cos_z, sin_z = dft_tables(LZ, 0, KZ, NZ)
    freq = lax.broadcasted_iota(jnp.int32, (KZ, 1), 0)
    weight = jnp.where((freq == 0) | (freq == LZ // 2), 1.0, 2.0) / (LX * LY * LZ)
    result = contract("vwk,ku->vwu", real_y, cos_z * weight)
    return result - contract("vwk,ku->vwu", imag_y, sin_z * weight)


def halo(block):
    count = lax.axis_size("space")
    up = [(i, i + 1) for i in range(count - 1)]
    down = [(i + 1, i) for i in range(count - 1)]
    low = lax.ppermute(block[-HALF:], "space", up)
    high = lax.ppermute(block[:HALF], "space", down)
    return jnp.concatenate([low, block, high], axis=0)


def fetch(templates, wanted):
    bank = templates.shape[0]
    count = lax.axis_size("space")
    me = lax.axis_index("space")
    owner = wanted // bank
    held = lax.dynamic_index_in_dim(templates, wanted % bank, 0, keepdims=False)
    step = 1
    while step < count:
        other = lax.ppermute(held, "space", [(i, i ^ step) for i in range(count)])
        mine = ((me ^ owner) & step) == 0
        held = jnp.where(mine, held, other)
        step *= 2
    return held


def shards(tomogram, templates, rot_ids):
    count_x = tomogram.shape[0]
    shared = fetch(templates, rot_ids[0])
    extended = halo(tomogram).reshape(count_x + TS, NY, NZ)
    tile_real, tile_imag = forward(extended, HALF)
    window = box_sum(extended * extended, count_x)
    inverse_norm = 1.0 / jnp.sqrt(window + TS**3 * 1e-06)
    normed = standardize(shared).reshape(TS, TS, TS)
    templ_real, templ_imag = forward(normed, 0)
    prod_real = tile_real * templ_real + tile_imag * templ_imag
    prod_imag = tile_imag * templ_real - tile_real * templ_imag
    scores = inverse(prod_real, prod_imag, count_x) * inverse_norm
    parts = lax.axis_size("rot")
    width = NY * NZ // parts
    blocks = scores.reshape(count_x, parts, width).transpose(1, 0, 2)
    gathered = lax.all_to_all(blocks, "rot", 0, 0)
    best = jnp.max(gathered, axis=0)
    total = jnp.sum(jnp.exp(sharpness * gathered), axis=0)
    return (best, jnp.log(total) / sharpness)


def solution(mesh):
    return jax.shard_map(
        shards,
        mesh=mesh,
        in_specs=(P("space", None), P("space", None), P("rot")),
        out_specs=(P("space", "rot"), P("space", "rot")),
        check_vma=False,
    )
```

```python
import functools
import math

import jax
import jax.numpy as jnp
import numpy as np
from jax import lax
from jax.experimental import pallas as pl
from jax.experimental.pallas import tpu as pltpu
from jax.sharding import PartitionSpec as P

NY = 64
NZ = 96
TS = 32
HALF = TS // 2
LY = NY + HALF
LZ = NZ + HALF
KZ = LZ // 2 + 1
LANES = 128
MID = LANES // 2

sharpness = 0.4


def angles(length, rows, columns):
    return (np.outer(rows, columns) % length) * (2.0 * math.pi / length)


def halves(table):
    high = np.asarray(table, np.float32).astype(jnp.bfloat16)
    low = (np.asarray(table, np.float64) - high.astype(np.float64)).astype(jnp.bfloat16)
    return high, low


def forward_z(first, count):
    turn = angles(LZ, np.arange(count) + first, np.arange(KZ))
    table = np.zeros((count, LANES))
    table[:, :KZ] = np.cos(turn)
    table[:, MID : MID + KZ] = -np.sin(turn)
    return table


def forward_y(positions):
    turn = angles(LY, np.arange(LY), positions)
    return np.concatenate([np.cos(turn), np.sin(turn)], axis=0)


def inverse_y(order):
    turn = angles(LY, order, np.arange(LY))
    return np.concatenate([np.cos(turn), np.sin(turn)], axis=0)


def inverse_z():
    turn = angles(LZ, np.arange(KZ), np.arange(NZ))
    weight = np.where((np.arange(KZ) == 0) | (np.arange(KZ) == LZ // 2), 1.0, 2.0) / (LY * LZ)
    table = np.zeros((LANES, NZ))
    table[:KZ] = np.cos(turn) * weight[:, None]
    table[MID : MID + KZ] = -np.sin(turn) * weight[:, None]
    return table


def band(count):
    offset = np.arange(count)[:, None] + HALF - np.arange(count)[None, :]
    return ((offset >= 0) & (offset < TS)).astype(np.float64)


def stacked_left(table):
    high, low = halves(table)
    return np.concatenate([high, high, low], axis=1)


def placed(table, parts):
    rows, columns = table.shape
    out = np.zeros((parts * rows, parts * columns))
    for part in range(parts):
        out[part * rows : (part + 1) * rows, part * columns : (part + 1) * columns] = table
    return out


def split(values):
    high = values.astype(jnp.bfloat16)
    low = (values - high.astype(jnp.float32)).astype(jnp.bfloat16)
    return high, low


def dot(left, right):
    return jnp.dot(left, right, preferred_element_type=jnp.float32)


def dot_right(values, high_table, low_table):
    high, low = split(values)
    return dot(high, high_table) + dot(low, high_table) + dot(high, low_table)


def dot_left(stack, values):
    high, low = split(values)
    return dot(stack, jnp.concatenate([high, low, high], axis=0))


def sign():
    lane = lax.broadcasted_iota(jnp.int32, (1, LANES), 1)
    return jnp.where(lane < MID, 1.0, -1.0).astype(jnp.float32)


def swapped(values):
    return pltpu.roll(values, MID, 1)


PLANES = 8


def volume_kernel(field, z_high, z_low, y_table, y_band, z_band, spectrum, norm, summed):
    count = field.shape[0]
    flip = sign()

    def planes(step, carry):
        start = step * PLANES
        block = field[pl.ds(start, PLANES)].reshape(PLANES * NY, NZ)
        along_z = dot_right(block, z_high[...], z_low[...])
        for pair in range(0, PLANES, 2):
            two = [along_z[(pair + i) * NY : (pair + i + 1) * NY] for i in range(2)]
            both = dot_left(y_table[...], jnp.concatenate(two, axis=1))
            for i in range(2):
                part = both[:, i * LANES : (i + 1) * LANES]
                spectrum[start + pair + i] = part[:LY] + swapped(part[LY:]) * flip
        return carry

    lax.fori_loop(0, count // PLANES, planes, 0)

    def rows(step, carry):
        at = pl.ds(pl.multiple_of(step * 8, 8), 8)
        level = [field[x, at, :] for x in range(count)]
        level = [value * value for value in level]
        width = 1
        while width < TS:
            level = [level[x] + level[x + width] for x in range(len(level) - width)]
            width *= 2
        for x in range(count - TS):
            summed[x, at, :] = level[x]
        return carry

    lax.fori_loop(0, NY // 8, rows, 0)

    out = count - TS
    parts = y_band.shape[0] // out
    along_y = []
    for x in range(out):
        high, low = split(summed[x])
        along_y.append(dot(y_band[...], jnp.concatenate([high, low], axis=0)))
    rows_of = y_band.shape[0] // parts
    total = None
    for part in range(parts):
        piece = [value[part * rows_of : (part + 1) * rows_of] for value in along_y]
        high, low = split(jnp.concatenate(piece, axis=0))
        table = z_band[part * NZ : (part + 1) * NZ, :]
        term = dot(high, table) + dot(low, table)
        total = term if total is None else total + term
    norm[...] = 1.0 / jnp.sqrt(total + TS**3 * 1e-06)


def template_kernel(
    template, spectrum, norm, z_high, z_low, y_table, back_y, back_high, back_low, scores, same, cross, product
):
    flip = sign()
    first = flip > 0
    values = template[...].astype(jnp.float32)
    size = values.shape[0] * values.shape[1]
    centred = values - jnp.sum(values) / size
    normed = centred / jnp.sqrt(jnp.sum(centred * centred) / size + 1e-06)
    along_z = dot_right(normed, z_high[...], z_low[...])
    groups = along_z.shape[1] // LANES
    deep = TS // groups

    def tap(a):
        rows = along_z[a * deep : (a + 1) * deep]
        return jnp.concatenate([rows[:, j * LANES : (j + 1) * LANES] for j in range(groups)], axis=0)

    for a in range(0, TS, 2):
        both = dot_left(y_table[...], jnp.concatenate([tap(a), tap(a + 1)], axis=1))
        for i in range(2):
            part = both[:, i * LANES : (i + 1) * LANES]
            value = part[:LY] + swapped(part[LY:]) * flip
            turned = swapped(value)
            same[a + i] = jnp.where(first, value, turned)
            cross[a + i] = jnp.where(first, -turned, value)

    out = spectrum.shape[0] - TS

    def rows(step, carry):
        at = pl.ds(pl.multiple_of(step * 8, 8), 8)
        plane = [spectrum[x, at, :] for x in range(out + TS - 1)]
        straight = [None] * out
        turned = [None] * out
        for a in range(TS):
            left, right = same[a, at, :], cross[a, at, :]
            for x in range(out):
                one, two = plane[x + a] * left, plane[x + a] * right
                straight[x] = one if a == 0 else straight[x] + one
                turned[x] = two if a == 0 else turned[x] + two
        for x in range(out):
            product[x, at, :] = straight[x] + swapped(turned[x])
        return carry

    lax.fori_loop(0, LY // 8, rows, 0)

    fields = []
    for x in range(0, out, 2):
        both = dot_left(back_y[...], jnp.concatenate([product[x], product[x + 1]], axis=1))
        for i in range(2):
            part = both[:, i * LANES : (i + 1) * LANES]
            fields.append(part[:NY] - swapped(part[NY:]) * flip)
    parts = back_high.shape[0] // LANES
    rows_of = NY // parts
    columns = [
        jnp.concatenate([value[j * rows_of : (j + 1) * rows_of] for value in fields], axis=0) for j in range(parts)
    ]
    result = dot_right(jnp.concatenate(columns, axis=1), back_high[...], back_low[...]) * norm[...]
    for x in range(out):
        scores[:, x, :] = result[x * rows_of : (x + 1) * rows_of]


def volume_side(field, parts):
    count = field.shape[0]
    out = count - TS
    rows_of = NY // parts
    order = np.arange(NY).reshape(rows_of, parts).T.reshape(-1)
    y_band = band(NY).T[order].astype(jnp.bfloat16)
    tables = (
        *halves(forward_z(HALF, NZ)),
        stacked_left(forward_y(np.arange(NY) + HALF)),
        np.concatenate([y_band, y_band], axis=1),
        placed(band(NZ), parts).astype(jnp.bfloat16),
    )
    return pl.pallas_call(
        volume_kernel,
        out_shape=(
            jax.ShapeDtypeStruct((count, LY, LANES), jnp.float32),
            jax.ShapeDtypeStruct((out * rows_of, parts * NZ), jnp.float32),
        ),
        scratch_shapes=[pltpu.VMEM((out, NY, NZ), jnp.float32)],
        compiler_params=pltpu.CompilerParams(vmem_limit_bytes=24 * 2**20),
        cost_estimate=pl.CostEstimate(flops=3 * 10**9, bytes_accessed=4 * 10**6, transcendentals=0),
        name="volume_side",
    )(field, *[jnp.asarray(table) for table in tables])


def template_side(template, spectrum, norm, parts):
    count = spectrum.shape[0]
    out = count - TS
    rows_of = NY // parts
    groups = LANES // TS
    order = np.arange(NY).reshape(rows_of, parts).T.reshape(-1)
    taps = np.arange(TS).reshape(TS // groups, groups).T.reshape(-1)
    tables = (
        *halves(placed(forward_z(0, TS), groups)),
        stacked_left(forward_y(taps)),
        stacked_left(inverse_y(order)),
        *halves(placed(inverse_z(), parts)),
    )
    return pl.pallas_call(
        template_kernel,
        out_shape=jax.ShapeDtypeStruct((rows_of, out, parts * NZ), jnp.float32),
        scratch_shapes=[
            pltpu.VMEM((TS, LY, LANES), jnp.float32),
            pltpu.VMEM((TS, LY, LANES), jnp.float32),
            pltpu.VMEM((out, LY, LANES), jnp.float32),
        ],
        compiler_params=pltpu.CompilerParams(vmem_limit_bytes=24 * 2**20),
        cost_estimate=pl.CostEstimate(flops=3 * 10**9, bytes_accessed=4 * 10**6, transcendentals=0),
        name="template_side",
    )(template, spectrum, norm, *[jnp.asarray(table) for table in tables])


def halo(block):
    count = lax.axis_size("space")
    up = [(i, i + 1) for i in range(count - 1)]
    down = [(i + 1, i) for i in range(count - 1)]
    low = lax.ppermute(block[-HALF:], "space", up)
    high = lax.ppermute(block[:HALF], "space", down)
    return jnp.concatenate([low, block, high], axis=0)


def fetch(templates, wanted):
    bank = templates.shape[0]
    count = lax.axis_size("space")
    me = lax.axis_index("space")
    owner = wanted // bank
    held = lax.dynamic_index_in_dim(templates, wanted % bank, 0, keepdims=False)
    step = 1
    while step < count:
        other = lax.ppermute(held, "space", [(i, i ^ step) for i in range(count)])
        mine = ((me ^ owner) & step) == 0
        held = jnp.where(mine, held, other)
        step *= 2
    return held


def shards(tomogram, templates, rot_ids):
    count_x = tomogram.shape[0]
    parts = lax.axis_size("rot")
    shared = fetch(templates, rot_ids[0])
    extended = halo(tomogram).reshape(count_x + TS, NY, NZ)
    spectrum, norm = volume_side(extended, NY // parts)
    blocks = template_side(shared.reshape(-1, LANES), spectrum, norm, NY // parts)
    gathered = lax.all_to_all(blocks, "rot", 0, 0)
    best = jnp.max(gathered, axis=0)
    total = jnp.sum(jnp.exp(sharpness * gathered), axis=0)
    return (best, jnp.log(total) / sharpness)


def solution(mesh):
    return jax.shard_map(
        shards,
        mesh=mesh,
        in_specs=(P("space", None), P("space", None), P("rot")),
        out_specs=(P("space", "rot"), P("space", "rot")),
        check_vma=False,
    )
```

```python
import functools
import math

import jax
import jax.numpy as jnp
import numpy as np
from jax import lax
from jax.experimental import pallas as pl
from jax.experimental.pallas import tpu as pltpu
from jax.sharding import PartitionSpec as P

NY = 64
NZ = 96
TS = 32
HALF = TS // 2
LY = NY + HALF
LZ = NZ + HALF
KZ = LZ // 2 + 1
LANES = 128
MID = LANES // 2

sharpness = 0.4
SENT = 256.0


def angles(length, rows, columns):
    return (np.outer(rows, columns) % length) * (2.0 * math.pi / length)


def halves(table):
    high = np.asarray(table, np.float32).astype(jnp.bfloat16)
    low = (np.asarray(table, np.float64) - high.astype(np.float64)).astype(jnp.bfloat16)
    return high, low


def forward_z(first, count):
    turn = angles(LZ, np.arange(count) + first, np.arange(KZ))
    table = np.zeros((count, LANES))
    table[:, :KZ] = np.cos(turn)
    table[:, MID : MID + KZ] = -np.sin(turn)
    return table


def forward_y(positions):
    turn = angles(LY, np.arange(LY), positions)
    return np.concatenate([np.cos(turn), np.sin(turn)], axis=0)


def inverse_y(order):
    turn = angles(LY, order, np.arange(LY))
    return np.concatenate([np.cos(turn), np.sin(turn)], axis=0)


def inverse_z():
    turn = angles(LZ, np.arange(KZ), np.arange(NZ))
    weight = np.where((np.arange(KZ) == 0) | (np.arange(KZ) == LZ // 2), 1.0, 2.0) / (LY * LZ)
    table = np.zeros((LANES, NZ))
    table[:KZ] = np.cos(turn) * weight[:, None]
    table[MID : MID + KZ] = -np.sin(turn) * weight[:, None]
    return table


def band(count):
    offset = np.arange(count)[:, None] + HALF - np.arange(count)[None, :]
    return ((offset >= 0) & (offset < TS)).astype(np.float64)


def stacked_left(table):
    high, low = halves(table)
    return np.concatenate([high, high, low], axis=1)


def placed(table, parts):
    rows, columns = table.shape
    out = np.zeros((parts * rows, parts * columns))
    for part in range(parts):
        out[part * rows : (part + 1) * rows, part * columns : (part + 1) * columns] = table
    return out


def split(values):
    high = values.astype(jnp.bfloat16)
    low = (values - high.astype(jnp.float32)).astype(jnp.bfloat16)
    return high, low


def dot(left, right):
    return jnp.dot(left, right, preferred_element_type=jnp.float32)


def dot_right(values, high_table, low_table):
    high, low = split(values)
    return dot(high, high_table) + dot(low, high_table) + dot(high, low_table)


def dot_left(stack, values):
    high, low = split(values)
    return dot(stack, jnp.concatenate([high, low, high], axis=0))


def sign():
    lane = lax.broadcasted_iota(jnp.int32, (1, LANES), 1)
    return jnp.where(lane < MID, 1.0, -1.0).astype(jnp.float32)


def swapped(values):
    return pltpu.roll(values, MID, 1)


PLANES = 8


def volume_kernel(field, z_high, z_low, y_table, y_band, z_band, spectrum, norm, summed):
    count = field.shape[0]
    flip = sign()

    def planes(step, carry):
        start = step * PLANES
        block = field[pl.ds(start, PLANES)].reshape(PLANES * NY, NZ)
        along_z = dot_right(block, z_high[...], z_low[...])
        for pair in range(0, PLANES, 2):
            two = [along_z[(pair + i) * NY : (pair + i + 1) * NY] for i in range(2)]
            both = dot_left(y_table[...], jnp.concatenate(two, axis=1))
            for i in range(2):
                part = both[:, i * LANES : (i + 1) * LANES]
                spectrum[start + pair + i] = part[:LY] + swapped(part[LY:]) * flip
        return carry

    lax.fori_loop(0, count // PLANES, planes, 0)

    def rows(step, carry):
        at = pl.ds(pl.multiple_of(step * 8, 8), 8)
        level = [field[x, at, :] for x in range(count)]
        level = [value * value for value in level]
        width = 1
        while width < TS:
            level = [level[x] + level[x + width] for x in range(len(level) - width)]
            width *= 2
        for x in range(count - TS):
            summed[x, at, :] = level[x]
        return carry

    lax.fori_loop(0, NY // 8, rows, 0)

    out = count - TS
    parts = y_band.shape[0] // out
    along_y = []
    for x in range(out):
        high, low = split(summed[x])
        along_y.append(dot(y_band[...], jnp.concatenate([high, low], axis=0)))
    rows_of = y_band.shape[0] // parts
    total = None
    for part in range(parts):
        piece = [value[part * rows_of : (part + 1) * rows_of] for value in along_y]
        high, low = split(jnp.concatenate(piece, axis=0))
        table = z_band[part * NZ : (part + 1) * NZ, :]
        term = dot(high, table) + dot(low, table)
        total = term if total is None else total + term
    norm[...] = 1.0 / jnp.sqrt(total + TS**3 * 1e-06)


def template_kernel(
    template, spectrum, norm, z_high, z_low, y_table, back_y, back_high, back_low, scores, same, cross, product
):
    flip = sign()
    first = flip > 0
    values = template[...].astype(jnp.float32)
    size = values.shape[0] * values.shape[1]
    centred = values - jnp.sum(values) / size
    normed = centred / jnp.sqrt(jnp.sum(centred * centred) / size + 1e-06)
    along_z = dot_right(normed, z_high[...], z_low[...])
    groups = along_z.shape[1] // LANES
    deep = TS // groups

    def tap(a):
        rows = along_z[a * deep : (a + 1) * deep]
        return jnp.concatenate([rows[:, j * LANES : (j + 1) * LANES] for j in range(groups)], axis=0)

    for a in range(0, TS, 2):
        both = dot_left(y_table[...], jnp.concatenate([tap(a), tap(a + 1)], axis=1))
        for i in range(2):
            part = both[:, i * LANES : (i + 1) * LANES]
            value = part[:LY] + swapped(part[LY:]) * flip
            turned = swapped(value)
            same[a + i] = jnp.where(first, value, turned)
            cross[a + i] = jnp.where(first, -turned, value)

    out = spectrum.shape[0] - TS

    def rows(step, carry):
        at = pl.ds(pl.multiple_of(step * 8, 8), 8)
        plane = [spectrum[x, at, :] for x in range(out + TS - 1)]
        straight = [None] * out
        turned = [None] * out
        for a in range(TS):
            left, right = same[a, at, :], cross[a, at, :]
            for x in range(out):
                one, two = plane[x + a] * left, plane[x + a] * right
                straight[x] = one if a == 0 else straight[x] + one
                turned[x] = two if a == 0 else turned[x] + two
        for x in range(out):
            product[x, at, :] = straight[x] + swapped(turned[x])
        return carry

    lax.fori_loop(0, LY // 8, rows, 0)

    fields = []
    for x in range(0, out, 2):
        both = dot_left(back_y[...], jnp.concatenate([product[x], product[x + 1]], axis=1))
        for i in range(2):
            part = both[:, i * LANES : (i + 1) * LANES]
            fields.append(part[:NY] - swapped(part[NY:]) * flip)
    parts = back_high.shape[0] // LANES
    rows_of = NY // parts
    columns = [
        jnp.concatenate([value[j * rows_of : (j + 1) * rows_of] for value in fields], axis=0) for j in range(parts)
    ]
    result = dot_right(jnp.concatenate(columns, axis=1), back_high[...], back_low[...]) * norm[...]
    for x in range(out):
        scores[:, x, :] = result[x * rows_of : (x + 1) * rows_of]


def volume_side(field, parts):
    count = field.shape[0]
    out = count - TS
    rows_of = NY // parts
    order = np.arange(NY).reshape(rows_of, parts).T.reshape(-1)
    y_band = band(NY).T[order].astype(jnp.bfloat16)
    tables = (
        *halves(forward_z(HALF, NZ)),
        stacked_left(forward_y(np.arange(NY) + HALF)),
        np.concatenate([y_band, y_band], axis=1),
        placed(band(NZ), parts).astype(jnp.bfloat16),
    )
    return pl.pallas_call(
        volume_kernel,
        out_shape=(
            jax.ShapeDtypeStruct((count, LY, LANES), jnp.float32),
            jax.ShapeDtypeStruct((out * rows_of, parts * NZ), jnp.float32),
        ),
        scratch_shapes=[pltpu.VMEM((out, NY, NZ), jnp.float32)],
        compiler_params=pltpu.CompilerParams(vmem_limit_bytes=24 * 2**20),
        cost_estimate=pl.CostEstimate(flops=3 * 10**9, bytes_accessed=4 * 10**6, transcendentals=0),
        name="volume_side",
    )(field, *[jnp.asarray(table) for table in tables])


def template_side(template, spectrum, norm, parts):
    count = spectrum.shape[0]
    out = count - TS
    rows_of = NY // parts
    groups = LANES // TS
    order = np.arange(NY).reshape(rows_of, parts).T.reshape(-1)
    taps = np.arange(TS).reshape(TS // groups, groups).T.reshape(-1)
    tables = (
        *halves(placed(forward_z(0, TS), groups)),
        stacked_left(forward_y(taps)),
        stacked_left(inverse_y(order)),
        *halves(placed(inverse_z(), parts)),
    )
    return pl.pallas_call(
        template_kernel,
        out_shape=jax.ShapeDtypeStruct((rows_of, out, parts * NZ), jnp.float32),
        scratch_shapes=[
            pltpu.VMEM((TS, LY, LANES), jnp.float32),
            pltpu.VMEM((TS, LY, LANES), jnp.float32),
            pltpu.VMEM((out, LY, LANES), jnp.float32),
        ],
        compiler_params=pltpu.CompilerParams(vmem_limit_bytes=24 * 2**20),
        cost_estimate=pl.CostEstimate(flops=3 * 10**9, bytes_accessed=4 * 10**6, transcendentals=0),
        name="template_side",
    )(template, spectrum, norm, *[jnp.asarray(table) for table in tables])


def doubling(held, owner, step):
    count = lax.axis_size("space")
    other = lax.ppermute(held, "space", [(i, i ^ step) for i in range(count)])
    mine = ((lax.axis_index("space") ^ owner) & step) == 0
    return jnp.where(mine, held, other)


def shards(tomogram, templates, rot_ids):
    count_x = tomogram.shape[0]
    parts = lax.axis_size("rot")
    count = lax.axis_size("space")
    bank = templates.shape[0]
    wanted = rot_ids[0]
    owner = wanted // bank
    held = lax.dynamic_index_in_dim(templates, wanted % bank, 0, keepdims=False)
    low = lax.ppermute(tomogram[-HALF:], "space", [(i, i + 1) for i in range(count - 1)])
    high = lax.ppermute(tomogram[:HALF], "space", [(i + 1, i) for i in range(count - 1)])
    steps = [1 << bit for bit in range((count - 1).bit_length())]
    for place, step in enumerate(steps):
        if place == len(steps) - 2:
            held, low = lax.optimization_barrier((held, low))
        if place == len(steps) - 1:
            held, high = lax.optimization_barrier((held, high))
        held = doubling(held, owner, step)
    extended = jnp.concatenate([low, tomogram, high], axis=0).reshape(count_x + TS, NY, NZ)
    spectrum, norm = volume_side(extended, NY // parts)
    blocks = template_side(held.reshape(-1, LANES), spectrum, norm, NY // parts)
    gathered = lax.all_to_all((blocks * SENT).astype(jnp.float16), "rot", 0, 0)
    arrived = gathered.astype(jnp.float32) * (1.0 / SENT)
    best = jnp.max(arrived, axis=0)
    total = jnp.sum(jnp.exp(sharpness * arrived), axis=0)
    return (best, jnp.log(total) / sharpness)


def solution(mesh):
    return jax.shard_map(
        shards,
        mesh=mesh,
        in_specs=(P("space", None), P("space", None), P("rot")),
        out_specs=(P("space", "rot"), P("space", "rot")),
        check_vma=False,
    )
```

```python
import math

import jax
import jax.numpy as jnp
import numpy as np
from jax import lax
from jax.experimental import pallas as pl
from jax.experimental.pallas import tpu as pltpu
from jax.sharding import PartitionSpec as P

NY = 64
NZ = 96
TS = 32
HALF = TS // 2
LY = NY + HALF
LZ = NZ + HALF
KZ = LZ // 2 + 1
LANES = 128
MID = LANES // 2

sharpness = 0.4
SENT = 256.0
ROT_X = 4


def angles(length, rows, columns):
    return (np.outer(rows, columns) % length) * (2.0 * math.pi / length)


def halves(table):
    high = np.asarray(table, np.float32).astype(jnp.bfloat16)
    low = (np.asarray(table, np.float64) - high.astype(np.float64)).astype(jnp.bfloat16)
    return high, low


def forward_z(first, count):
    turn = angles(LZ, np.arange(count) + first, np.arange(KZ))
    table = np.zeros((count, LANES))
    table[:, :KZ] = np.cos(turn)
    table[:, MID : MID + KZ] = -np.sin(turn)
    return table


def forward_y(positions):
    turn = angles(LY, np.arange(LY), positions)
    return np.concatenate([np.cos(turn), np.sin(turn)], axis=0)


def inverse_y(order):
    turn = angles(LY, order, np.arange(LY))
    return np.concatenate([np.cos(turn), np.sin(turn)], axis=0)


def inverse_z():
    turn = angles(LZ, np.arange(KZ), np.arange(NZ))
    weight = np.where((np.arange(KZ) == 0) | (np.arange(KZ) == LZ // 2), 1.0, 2.0) / (LY * LZ)
    table = np.zeros((LANES, NZ))
    table[:KZ] = np.cos(turn) * weight[:, None]
    table[MID : MID + KZ] = -np.sin(turn) * weight[:, None]
    return table


def band(count):
    offset = np.arange(count)[:, None] + HALF - np.arange(count)[None, :]
    return ((offset >= 0) & (offset < TS)).astype(np.float64)


def stacked_left(table):
    high, low = halves(table)
    return np.concatenate([high, high, low], axis=1)


def placed(table, parts):
    rows, columns = table.shape
    out = np.zeros((parts * rows, parts * columns))
    for part in range(parts):
        out[part * rows : (part + 1) * rows, part * columns : (part + 1) * columns] = table
    return out


def split(values):
    high = values.astype(jnp.bfloat16)
    low = (values - high.astype(jnp.float32)).astype(jnp.bfloat16)
    return high, low


def dot(left, right):
    return jnp.dot(left, right, preferred_element_type=jnp.float32)


def dot_right(values, high_table, low_table):
    high, low = split(values)
    return dot(high, high_table) + dot(low, high_table) + dot(high, low_table)


def dot_left(stack, values):
    high, low = split(values)
    return dot(stack, jnp.concatenate([high, low, high], axis=0))


def sign():
    lane = lax.broadcasted_iota(jnp.int32, (1, LANES), 1)
    return jnp.where(lane < MID, 1.0, -1.0).astype(jnp.float32)


def swapped(values):
    return pltpu.roll(values, MID, 1)


PLANES = 8


def transform(field, spectrum, base, z_high, z_low, y_table):
    flip = sign()

    def planes(step, carry):
        start = step * PLANES
        block = field[pl.ds(start, PLANES)].reshape(PLANES * NY, NZ)
        along_z = dot_right(block, z_high[...], z_low[...])
        for pair in range(0, PLANES, 2):
            two = [along_z[(pair + i) * NY : (pair + i + 1) * NY] for i in range(2)]
            both = dot_left(y_table[...], jnp.concatenate(two, axis=1))
            for i in range(2):
                part = both[:, i * LANES : (i + 1) * LANES]
                spectrum[base + start + pair + i] = part[:LY] + swapped(part[LY:]) * flip
        return carry

    lax.fori_loop(0, field.shape[0] // PLANES, planes, 0)


def volume_kernel(odd, own, near, far, z_high, z_low, y_table, y_band, z_band, spectrum, norm, summed):
    count = own.shape[0]
    is_odd = odd[0] == 1
    low = jnp.where(is_odd, 0, 2 * count)
    for field, base in ((own, count), (near, low), (far, 2 * count - low)):
        transform(field, spectrum, base, z_high, z_low, y_table)

    def rows(step, carry):
        at = pl.ds(pl.multiple_of(step * 8, 8), 8)
        below, above = [], []
        for x in range(count):
            one, two = near[x, at, :], far[x, at, :]
            below.append(jnp.where(is_odd, one, two))
            above.append(jnp.where(is_odd, two, one))
        level = [value * value for value in below + [own[x, at, :] for x in range(count)] + above]
        width = 1
        while width < TS:
            level = [level[x] + level[x + width] for x in range(len(level) - width)]
            width *= 2
        for x in range(count):
            summed[x, at, :] = level[x]
        return carry

    lax.fori_loop(0, NY // 8, rows, 0)

    parts = y_band.shape[0] // count
    along_y = []
    for x in range(count):
        high, low = split(summed[x])
        along_y.append(dot(y_band[...], jnp.concatenate([high, low], axis=0)))
    rows_of = y_band.shape[0] // parts
    total = None
    for part in range(parts):
        piece = [value[part * rows_of : (part + 1) * rows_of] for value in along_y]
        high, low = split(jnp.concatenate(piece, axis=0))
        table = z_band[part * NZ : (part + 1) * NZ, :]
        term = dot(high, table) + dot(low, table)
        total = term if total is None else total + term
    norm[...] = 1.0 / jnp.sqrt(total + TS**3 * 1e-06)


def template_kernel(
    apart, held, four, eight, twelve, spectrum, norm, z_high, z_low, y_table, back_y, back_high, back_low, scores, same, cross, product
):
    flip = sign()
    first = flip > 0
    values = held[...].astype(jnp.float32)
    for step, other in ((4, four), (8, eight), (12, twelve)):
        values = jnp.where(apart[0] == step, other[...].astype(jnp.float32), values)
    size = values.shape[0] * values.shape[1]
    centred = values - jnp.sum(values) / size
    normed = centred / jnp.sqrt(jnp.sum(centred * centred) / size + 1e-06)
    along_z = dot_right(normed, z_high[...], z_low[...])
    groups = along_z.shape[1] // LANES
    deep = TS // groups

    def tap(a):
        rows = along_z[a * deep : (a + 1) * deep]
        return jnp.concatenate([rows[:, j * LANES : (j + 1) * LANES] for j in range(groups)], axis=0)

    for a in range(0, TS, 2):
        both = dot_left(y_table[...], jnp.concatenate([tap(a), tap(a + 1)], axis=1))
        for i in range(2):
            part = both[:, i * LANES : (i + 1) * LANES]
            value = part[:LY] + swapped(part[LY:]) * flip
            turned = swapped(value)
            same[a + i] = jnp.where(first, value, turned)
            cross[a + i] = jnp.where(first, -turned, value)

    out = spectrum.shape[0] - TS

    def rows(step, carry):
        at = pl.ds(pl.multiple_of(step * 8, 8), 8)
        plane = [spectrum[x, at, :] for x in range(out + TS - 1)]
        straight = [None] * out
        turned = [None] * out
        for a in range(TS):
            left, right = same[a, at, :], cross[a, at, :]
            for x in range(out):
                one, two = plane[x + a] * left, plane[x + a] * right
                straight[x] = one if a == 0 else straight[x] + one
                turned[x] = two if a == 0 else turned[x] + two
        for x in range(out):
            product[x, at, :] = straight[x] + swapped(turned[x])
        return carry

    lax.fori_loop(0, LY // 8, rows, 0)

    fields = []
    for x in range(0, out, 2):
        both = dot_left(back_y[...], jnp.concatenate([product[x], product[x + 1]], axis=1))
        for i in range(2):
            part = both[:, i * LANES : (i + 1) * LANES]
            fields.append(part[:NY] - swapped(part[NY:]) * flip)
    parts = back_high.shape[0] // LANES
    rows_of = NY // parts
    columns = [
        jnp.concatenate([value[j * rows_of : (j + 1) * rows_of] for value in fields], axis=0) for j in range(parts)
    ]
    result = dot_right(jnp.concatenate(columns, axis=1), back_high[...], back_low[...]) * norm[...]
    for x in range(out):
        scores[:, x, :] = result[x * rows_of : (x + 1) * rows_of]


def cost(flops):
    return pl.CostEstimate(flops=flops, bytes_accessed=4 * 10**6, transcendentals=0)


PARAMS = pltpu.CompilerParams(vmem_limit_bytes=24 * 2**20)
IN_VMEM = pl.BlockSpec(memory_space=pltpu.VMEM)
IN_SMEM = pl.BlockSpec(memory_space=pltpu.SMEM)


def volume_tables():
    return [*halves(forward_z(HALF, NZ)), stacked_left(forward_y(np.arange(NY) + HALF))]


def volume_side(odd, own, near, far, parts):
    count = own.shape[0]
    rows_of = NY // parts
    order = np.arange(NY).reshape(rows_of, parts).T.reshape(-1)
    y_band = band(NY).T[order].astype(jnp.bfloat16)
    tables = volume_tables() + [
        np.concatenate([y_band, y_band], axis=1),
        placed(band(NZ), parts).astype(jnp.bfloat16),
    ]
    return pl.pallas_call(
        volume_kernel,
        out_shape=(
            jax.ShapeDtypeStruct((3 * count, LY, LANES), jnp.float32),
            jax.ShapeDtypeStruct((count * rows_of, parts * NZ), jnp.float32),
        ),
        in_specs=[IN_SMEM] + [IN_VMEM] * 8,
        out_specs=(IN_VMEM, IN_VMEM),
        scratch_shapes=[pltpu.VMEM((count, NY, NZ), jnp.float32)],
        compiler_params=PARAMS,
        cost_estimate=cost(3 * 10**9),
        name="volume_side",
    )(odd, own, near, far, *[jnp.asarray(table) for table in tables])


def template_side(apart, candidates, spectrum, norm, parts):
    out = spectrum.shape[0] - TS
    rows_of = NY // parts
    groups = LANES // TS
    order = np.arange(NY).reshape(rows_of, parts).T.reshape(-1)
    taps = np.arange(TS).reshape(TS // groups, groups).T.reshape(-1)
    tables = (
        *halves(placed(forward_z(0, TS), groups)),
        stacked_left(forward_y(taps)),
        stacked_left(inverse_y(order)),
        *halves(placed(inverse_z(), parts)),
    )
    return pl.pallas_call(
        template_kernel,
        out_shape=jax.ShapeDtypeStruct((rows_of, out, parts * NZ), jnp.float32),
        in_specs=[IN_SMEM] + [IN_VMEM] * 12,
        out_specs=IN_VMEM,
        scratch_shapes=[
            pltpu.VMEM((TS, LY, LANES), jnp.float32),
            pltpu.VMEM((TS, LY, LANES), jnp.float32),
            pltpu.VMEM((out, LY, LANES), jnp.float32),
        ],
        compiler_params=PARAMS,
        cost_estimate=cost(3 * 10**9),
        name="template_side",
    )(apart, *candidates, spectrum, norm, *[jnp.asarray(table) for table in tables])


def join_kernel(scores, best, mass):
    top = scores[0]
    total = jnp.exp(sharpness * top)
    for index in range(1, scores.shape[0]):
        value = scores[index]
        top = jnp.maximum(top, value)
        total = total + jnp.exp(sharpness * value)
    best[...] = top
    mass[...] = jnp.log(total) / sharpness


def join(scores):
    shape = jax.ShapeDtypeStruct(scores.shape[1:], jnp.float32)
    return pl.pallas_call(
        join_kernel,
        out_shape=(shape, shape),
        in_specs=[IN_VMEM],
        out_specs=(IN_VMEM, IN_VMEM),
        compiler_params=PARAMS,
        name="join",
    )(scores)


def exchange(value, step):
    return lax.ppermute(value, "space", [(i, i ^ step) for i in range(lax.axis_size("space"))])


def next_slab(slab):
    count, copies = lax.axis_size("space"), lax.axis_size("rot")
    pairs = []
    for first in range(1, count - 1, 2):
        ahead = ROT_X if first % 4 == 3 else 0
        for copy in range(copies):
            one = first * copies + copy
            two = (first + 1) * copies + (copy + ahead) % copies
            pairs += [(one, two), (two, one)]
    return lax.ppermute(slab, ("space", "rot"), pairs)


def shards(tomogram, templates, rot_ids):
    parts = lax.axis_size("rot")
    me = lax.axis_index("space")
    bank = templates.shape[0]
    wanted = rot_ids[0]
    apart = me ^ (wanted // bank)
    held = lax.dynamic_index_in_dim(templates, wanted % bank, 0, keepdims=False)
    near = exchange(tomogram, 1)
    far = next_slab(tomogram)
    own = tomogram.reshape(-1, NY, NZ)
    held = jnp.where((apart & 1) == 0, held, exchange(held, 1))
    held, own = lax.optimization_barrier((held, own))
    held = jnp.where((apart & 2) == 0, held, exchange(held, 2))
    held, near = lax.optimization_barrier((held, near))
    candidates = [held] + [exchange(held, step) for step in (4, 8, 12)]
    near, far = near.reshape(-1, NY, NZ), far.reshape(-1, NY, NZ)
    spectrum, norm = volume_side((me & 1).reshape(1), own, near, far, NY // parts)
    candidates = [value.reshape(-1, LANES) for value in candidates]
    blocks = template_side((apart & 12).reshape(1), candidates, spectrum, norm, NY // parts)
    arrived = lax.all_to_all((blocks * SENT).astype(jnp.float16), "rot", 0, 0)
    return join(arrived.astype(jnp.float32) * (1.0 / SENT))


def solution(mesh):
    return jax.shard_map(
        shards,
        mesh=mesh,
        in_specs=(P("space", None), P("space", None), P("rot")),
        out_specs=(P("space", "rot"), P("space", "rot")),
        check_vma=False,
    )
```

```python
import functools
import math

import jax
import jax.numpy as jnp
import numpy as np
from jax import lax
from jax.experimental import pallas as pl
from jax.experimental.pallas import tpu as pltpu
from jax.sharding import PartitionSpec as P

NY = 64
NZ = 96
TS = 32
HALF = TS // 2
LY = NY + HALF
LZ = NZ + HALF
KZ = LZ // 2 + 1
LANES = 128
MID = LANES // 2

sharpness = 0.4
SENT = 256.0
ROT_X = 4


def angles(length, rows, columns):
    return (np.outer(rows, columns) % length) * (2.0 * math.pi / length)


def halves(table):
    high = np.asarray(table, np.float32).astype(jnp.bfloat16)
    low = (np.asarray(table, np.float64) - high.astype(np.float64)).astype(jnp.bfloat16)
    return high, low


def forward_z(first, count):
    turn = angles(LZ, np.arange(count) + first, np.arange(KZ))
    table = np.zeros((count, LANES))
    table[:, :KZ] = np.cos(turn)
    table[:, MID : MID + KZ] = -np.sin(turn)
    return table


def forward_y(positions):
    turn = angles(LY, np.arange(LY), positions)
    return np.concatenate([np.cos(turn), np.sin(turn)], axis=0)


def inverse_y(order):
    turn = angles(LY, order, np.arange(LY))
    return np.concatenate([np.cos(turn), np.sin(turn)], axis=0)


def inverse_z():
    turn = angles(LZ, np.arange(KZ), np.arange(NZ))
    weight = np.where((np.arange(KZ) == 0) | (np.arange(KZ) == LZ // 2), 1.0, 2.0) / (LY * LZ)
    table = np.zeros((LANES, NZ))
    table[:KZ] = np.cos(turn) * weight[:, None]
    table[MID : MID + KZ] = -np.sin(turn) * weight[:, None]
    return table


def band(count):
    offset = np.arange(count)[:, None] + HALF - np.arange(count)[None, :]
    return ((offset >= 0) & (offset < TS)).astype(np.float64)


def stacked_left(table):
    high, low = halves(table)
    return np.concatenate([high, high, low], axis=1)


def placed(table, parts):
    rows, columns = table.shape
    out = np.zeros((parts * rows, parts * columns))
    for part in range(parts):
        out[part * rows : (part + 1) * rows, part * columns : (part + 1) * columns] = table
    return out


def wide_right(table):
    high, low = halves(table)
    rows = np.zeros((LANES - table.shape[0], 2 * table.shape[1]), high.dtype)
    first = np.concatenate([high, low], axis=1)
    second = np.concatenate([high, np.zeros_like(high)], axis=1)
    return np.concatenate([first, rows, second, rows], axis=0)


def split(values):
    high = values.astype(jnp.bfloat16)
    low = (values - high.astype(jnp.float32)).astype(jnp.bfloat16)
    return high, low


def dot(left, right):
    return jnp.dot(left, right, preferred_element_type=jnp.float32)


def dot_right(values, high_table, low_table):
    high, low = split(values)
    return dot(high, high_table) + dot(low, high_table) + dot(high, low_table)


def dot_wide(values, table):
    high, low = split(values)
    blank = [jnp.zeros((values.shape[0], LANES - values.shape[1]), jnp.bfloat16)] if values.shape[1] < LANES else []
    both = dot(jnp.concatenate([high, *blank, low, *blank], axis=1), table)
    return both[:, : both.shape[1] // 2] + both[:, both.shape[1] // 2 :]


def dot_left(stack, values):
    high, low = split(values)
    return dot(stack, jnp.concatenate([high, low, high], axis=0))


def sign():
    lane = lax.broadcasted_iota(jnp.int32, (1, LANES), 1)
    return jnp.where(lane < MID, 1.0, -1.0).astype(jnp.float32)


def swapped(values):
    return pltpu.roll(values, MID, 1)


PLANES = 16


def transform(field, spectrum, base, z_wide, y_table):
    flip = sign()

    def planes(step, carry):
        start = step * PLANES
        block = field[pl.ds(start, PLANES)].reshape(PLANES * NY, NZ)
        along_z = dot_wide(block, z_wide[...])
        for pair in range(0, PLANES, 2):
            two = [along_z[(pair + i) * NY : (pair + i + 1) * NY] for i in range(2)]
            both = dot_left(y_table[...], jnp.concatenate(two, axis=1))
            for i in range(2):
                part = both[:, i * LANES : (i + 1) * LANES]
                spectrum[base + start + pair + i] = part[:LY] + swapped(part[LY:]) * flip
        return carry

    lax.fori_loop(0, field.shape[0] // PLANES, planes, 0)


def volume_kernel(odd, own, near, far, z_wide, y_table, y_band, z_band, spectrum, norm, summed):
    count = own.shape[0]
    is_odd = odd[0] == 1
    low = jnp.where(is_odd, 0, 2 * count)
    for field, base in ((own, count), (near, low), (far, 2 * count - low)):
        transform(field, spectrum, base, z_wide, y_table)

    for step in range(NY // 8):
        at = pl.ds(step * 8, 8)
        below, above = [], []
        for x in range(count):
            one, two = near[x, at, :], far[x, at, :]
            below.append(jnp.where(is_odd, one, two))
            above.append(jnp.where(is_odd, two, one))
        level = [value * value for value in below + [own[x, at, :] for x in range(count)] + above]
        width = 1
        while width < TS:
            level = [level[x] + level[x + width] for x in range(len(level) - width)]
            width *= 2
        for x in range(count):
            summed[x, at, :] = level[x]

    parts = y_band.shape[0] // count
    along_y = []
    for x in range(count):
        high, low = split(summed[x])
        along_y.append(dot(y_band[...], jnp.concatenate([high, low], axis=0)))
    rows_of = y_band.shape[0] // parts
    total = None
    for part in range(parts):
        piece = [value[part * rows_of : (part + 1) * rows_of] for value in along_y]
        high, low = split(jnp.concatenate(piece, axis=0))
        table = z_band[part * NZ : (part + 1) * NZ, :]
        term = dot(high, table) + dot(low, table)
        total = term if total is None else total + term
    norm[...] = 1.0 / jnp.sqrt(total + TS**3 * 1e-06)


def slide(plane, taps, count):
    if count <= 2:
        return [functools.reduce(jnp.add, [plane[x + a] * tap for a, tap in enumerate(taps)]) for x in range(count)]
    half = count // 2
    need = half + len(taps) // 2 - 1
    even, odd = plane[0::2], plane[1::2]
    first, second = taps[0::2], taps[1::2]
    shared = slide(odd[:need], [one + two for one, two in zip(first, second)], half)
    low = slide([even[i] - odd[i] for i in range(need)], first, half)
    high = slide([even[i + 1] - odd[i] for i in range(need)], second, half)
    return [shared[x // 2] + (high if x % 2 else low)[x // 2] for x in range(count)]


def template_kernel(
    apart, held, four, eight, twelve, spectrum, norm, z_high, z_low, y_table, back_y, back_high, back_low, scores, same, cross, product
):
    flip = sign()
    first = flip > 0
    values = held[...].astype(jnp.float32)
    for step, other in ((4, four), (8, eight), (12, twelve)):
        values = jnp.where(apart[0] == step, other[...].astype(jnp.float32), values)
    size = values.shape[0] * values.shape[1]
    centred = values - jnp.sum(values) / size
    normed = centred / jnp.sqrt(jnp.sum(centred * centred) / size + 1e-06)
    along_z = dot_right(normed, z_high[...], z_low[...])
    groups = along_z.shape[1] // LANES
    deep = TS // groups

    def tap(a):
        rows = along_z[a * deep : (a + 1) * deep]
        return jnp.concatenate([rows[:, j * LANES : (j + 1) * LANES] for j in range(groups)], axis=0)

    for a in range(0, TS, 2):
        both = dot_left(y_table[...], jnp.concatenate([tap(a), tap(a + 1)], axis=1))
        for i in range(2):
            part = both[:, i * LANES : (i + 1) * LANES]
            value = part[:LY] + swapped(part[LY:]) * flip
            turned = swapped(value)
            same[a + i] = jnp.where(first, value, turned)
            cross[a + i] = jnp.where(first, -turned, value)

    out = spectrum.shape[0] - TS

    def rows(step, carry):
        at = pl.ds(pl.multiple_of(step * 8, 8), 8)
        plane = [spectrum[x, at, :] for x in range(out + TS)]
        straight = slide(plane, [same[a, at, :] for a in range(TS)], out)
        for x in range(out):
            product[x, at, :] = straight[x]
        turned = slide(plane, [cross[a, at, :] for a in range(TS)], out)
        for x in range(out):
            product[x, at, :] = product[x, at, :] + swapped(turned[x])
        return carry

    lax.fori_loop(0, LY // 8, rows, 0)

    fields = []
    for x in range(0, out, 2):
        both = dot_left(back_y[...], jnp.concatenate([product[x], product[x + 1]], axis=1))
        for i in range(2):
            part = both[:, i * LANES : (i + 1) * LANES]
            fields.append(part[:NY] - swapped(part[NY:]) * flip)
    parts = back_high.shape[0] // LANES
    rows_of = NY // parts
    columns = [
        jnp.concatenate([value[j * rows_of : (j + 1) * rows_of] for value in fields], axis=0) for j in range(parts)
    ]
    result = dot_right(jnp.concatenate(columns, axis=1), back_high[...], back_low[...]) * norm[...]
    for x in range(out):
        scores[:, x, :] = result[x * rows_of : (x + 1) * rows_of]


def cost(flops):
    return pl.CostEstimate(flops=flops, bytes_accessed=4 * 10**6, transcendentals=0)


PARAMS = pltpu.CompilerParams(vmem_limit_bytes=24 * 2**20)
IN_VMEM = pl.BlockSpec(memory_space=pltpu.VMEM)
IN_SMEM = pl.BlockSpec(memory_space=pltpu.SMEM)


def volume_tables():
    return [wide_right(forward_z(HALF, NZ)), stacked_left(forward_y(np.arange(NY) + HALF))]


def volume_side(odd, own, near, far, parts):
    count = own.shape[0]
    rows_of = NY // parts
    order = np.arange(NY).reshape(rows_of, parts).T.reshape(-1)
    y_band = band(NY).T[order].astype(jnp.bfloat16)
    tables = volume_tables() + [
        np.concatenate([y_band, y_band], axis=1),
        placed(band(NZ), parts).astype(jnp.bfloat16),
    ]
    return pl.pallas_call(
        volume_kernel,
        out_shape=(
            jax.ShapeDtypeStruct((3 * count, LY, LANES), jnp.float32),
            jax.ShapeDtypeStruct((count * rows_of, parts * NZ), jnp.float32),
        ),
        in_specs=[IN_SMEM] + [IN_VMEM] * 7,
        out_specs=(IN_VMEM, IN_VMEM),
        scratch_shapes=[pltpu.VMEM((count, NY, NZ), jnp.float32)],
        compiler_params=PARAMS,
        cost_estimate=cost(3 * 10**9),
        name="volume_side",
    )(odd, own, near, far, *[jnp.asarray(table) for table in tables])


def template_side(apart, candidates, spectrum, norm, parts):
    out = spectrum.shape[0] - TS
    rows_of = NY // parts
    groups = LANES // TS
    order = np.arange(NY).reshape(rows_of, parts).T.reshape(-1)
    taps = np.arange(TS).reshape(TS // groups, groups).T.reshape(-1)
    tables = (
        *halves(placed(forward_z(0, TS), groups)),
        stacked_left(forward_y(taps)),
        stacked_left(inverse_y(order)),
        *halves(placed(inverse_z(), parts)),
    )
    return pl.pallas_call(
        template_kernel,
        out_shape=jax.ShapeDtypeStruct((rows_of, out, parts * NZ), jnp.float32),
        in_specs=[IN_SMEM] + [IN_VMEM] * 12,
        out_specs=IN_VMEM,
        scratch_shapes=[
            pltpu.VMEM((TS, LY, LANES), jnp.float32),
            pltpu.VMEM((TS, LY, LANES), jnp.float32),
            pltpu.VMEM((out, LY, LANES), jnp.float32),
        ],
        compiler_params=PARAMS,
        cost_estimate=cost(3 * 10**9),
        name="template_side",
    )(apart, *candidates, spectrum, norm, *[jnp.asarray(table) for table in tables])


def join_kernel(scores, best, mass):
    top = scores[0]
    total = jnp.exp(sharpness * top)
    for index in range(1, scores.shape[0]):
        value = scores[index]
        top = jnp.maximum(top, value)
        total = total + jnp.exp(sharpness * value)
    best[...] = top
    mass[...] = jnp.log(total) / sharpness


def join(scores):
    shape = jax.ShapeDtypeStruct(scores.shape[1:], jnp.float32)
    return pl.pallas_call(
        join_kernel,
        out_shape=(shape, shape),
        in_specs=[IN_VMEM],
        out_specs=(IN_VMEM, IN_VMEM),
        compiler_params=PARAMS,
        name="join",
    )(scores)


def exchange(value, step):
    return lax.ppermute(value, "space", [(i, i ^ step) for i in range(lax.axis_size("space"))])


def next_slab(slab):
    count, copies = lax.axis_size("space"), lax.axis_size("rot")
    pairs = []
    for first in range(1, count - 1, 2):
        ahead = ROT_X if first % 4 == 3 else 0
        for copy in range(copies):
            one = first * copies + copy
            two = (first + 1) * copies + (copy + ahead) % copies
            pairs += [(one, two), (two, one)]
    return lax.ppermute(slab, ("space", "rot"), pairs)


def shards(tomogram, templates, rot_ids):
    parts = lax.axis_size("rot")
    me = lax.axis_index("space")
    bank = templates.shape[0]
    wanted = rot_ids[0]
    apart = me ^ (wanted // bank)
    held = lax.dynamic_index_in_dim(templates, wanted % bank, 0, keepdims=False)
    near = exchange(tomogram, 1)
    far = next_slab(tomogram)
    own = tomogram.reshape(-1, NY, NZ)
    held = jnp.where((apart & 1) == 0, held, exchange(held, 1))
    held, own = lax.optimization_barrier((held, own))
    held = jnp.where((apart & 2) == 0, held, exchange(held, 2))
    held, near = lax.optimization_barrier((held, near))
    candidates = [held] + [exchange(held, step) for step in (4, 8, 12)]
    near, far = near.reshape(-1, NY, NZ), far.reshape(-1, NY, NZ)
    spectrum, norm = volume_side((me & 1).reshape(1), own, near, far, NY // parts)
    candidates = [value.reshape(-1, LANES) for value in candidates]
    blocks = template_side((apart & 12).reshape(1), candidates, spectrum, norm, NY // parts)
    arrived = lax.all_to_all((blocks * SENT).astype(jnp.float16), "rot", 0, 0)
    return join(arrived.astype(jnp.float32) * (1.0 / SENT))


def solution(mesh):
    return jax.shard_map(
        shards,
        mesh=mesh,
        in_specs=(P("space", None), P("space", None), P("rot")),
        out_specs=(P("space", "rot"), P("space", "rot")),
        check_vma=False,
    )
```

```python
import functools
import math

import jax
import jax.numpy as jnp
import numpy as np
from jax import lax
from jax.experimental import pallas as pl
from jax.experimental.pallas import tpu as pltpu
from jax.sharding import PartitionSpec as P

NY = 64
NZ = 96
TS = 32
HALF = TS // 2
LY = NY + HALF
LZ = NZ + HALF
KZ = LZ // 2 + 1
LANES = 128
MID = LANES // 2

sharpness = 0.4
SENT = 256.0
SCALE = 8192.0
ROT_X = 4


def angles(length, rows, columns):
    return (np.outer(rows, columns) % length) * (2.0 * math.pi / length)


def halves(table):
    high = np.asarray(table, np.float32).astype(jnp.bfloat16)
    low = (np.asarray(table, np.float64) - high.astype(np.float64)).astype(jnp.bfloat16)
    return high, low


def forward_z(first, count):
    turn = angles(LZ, np.arange(count) + first, np.arange(KZ))
    table = np.zeros((count, LANES))
    table[:, :KZ] = np.cos(turn)
    table[:, MID : MID + KZ] = -np.sin(turn)
    return table


def forward_y(positions):
    turn = angles(LY, np.arange(LY), positions)
    return np.concatenate([np.cos(turn), np.sin(turn)], axis=0)


def inverse_y(order):
    turn = angles(LY, order, np.arange(LY))
    return np.concatenate([np.cos(turn), np.sin(turn)], axis=0)


def inverse_z():
    turn = angles(LZ, np.arange(KZ), np.arange(NZ))
    weight = np.where((np.arange(KZ) == 0) | (np.arange(KZ) == LZ // 2), 1.0, 2.0) / (LY * LZ)
    table = np.zeros((LANES, NZ))
    table[:KZ] = np.cos(turn) * weight[:, None]
    table[MID : MID + KZ] = -np.sin(turn) * weight[:, None]
    return table


def band(count):
    offset = np.arange(count)[:, None] + HALF - np.arange(count)[None, :]
    return ((offset >= 0) & (offset < TS)).astype(np.float64)


def stacked_left(table):
    high, low = halves(table)
    return np.concatenate([high, high, low], axis=1)


def wide_right(table):
    high, low = halves(table)
    rows = np.zeros((LANES - table.shape[0], 2 * table.shape[1]), high.dtype)
    first = np.concatenate([high, low], axis=1)
    second = np.concatenate([high, np.zeros_like(high)], axis=1)
    return np.concatenate([first, rows, second, rows], axis=0)


def split(values):
    high = values.astype(jnp.bfloat16)
    low = (values - high.astype(jnp.float32)).astype(jnp.bfloat16)
    return high, low


def dot(left, right):
    return jnp.dot(left, right, preferred_element_type=jnp.float32)


def dot_right(values, high_table, low_table):
    high, low = split(values)
    return dot(high, high_table) + dot(low, high_table) + dot(high, low_table)


def dot_wide(values, table):
    high, low = split(values)
    blank = [jnp.zeros((values.shape[0], LANES - values.shape[1]), jnp.bfloat16)] if values.shape[1] < LANES else []
    both = dot(jnp.concatenate([high, *blank, low, *blank], axis=1), table)
    return both[:, : both.shape[1] // 2] + both[:, both.shape[1] // 2 :]


def dot_left(stack, values):
    high, low = split(values)
    return dot(stack, jnp.concatenate([high, low, high], axis=0))


def lane_block(tile, part, parts):
    width = tile.shape[1] // parts
    lane = lax.broadcasted_iota(jnp.int32, (1, tile.shape[1]), 1)
    keep = (lane >= part * width) & (lane < (part + 1) * width)
    return tile * keep.astype(jnp.float32).astype(jnp.bfloat16)


def row_block(tile, part, parts):
    height = tile.shape[0] // parts
    row = lax.broadcasted_iota(jnp.int32, tile.shape, 0)
    keep = (row >= part * height) & (row < (part + 1) * height)
    return tile * keep.astype(jnp.float32).astype(jnp.bfloat16)


def lane_blocks(tile, parts):
    return jnp.concatenate([lane_block(tile, part, parts) for part in range(parts)], axis=0)


def row_blocks(tile, parts):
    return jnp.concatenate([row_block(tile, part, parts) for part in range(parts)], axis=1)


def sign():
    lane = lax.broadcasted_iota(jnp.int32, (1, LANES), 1)
    return jnp.where(lane < MID, 1.0, -1.0).astype(jnp.float32)


def swapped(values):
    return pltpu.roll(values, MID, 1)


PLANES = 16


def transform(field, spectrum, base, scale, z_wide, y_table):
    flip = sign()

    def planes(step, carry):
        start = step * PLANES
        block = field[pl.ds(start, PLANES)].reshape(PLANES * NY, NZ)
        along_z = dot_wide(block if scale is None else block * scale, z_wide[...])
        for pair in range(0, PLANES, 2):
            two = [along_z[(pair + i) * NY : (pair + i + 1) * NY] for i in range(2)]
            both = dot_left(y_table[...], jnp.concatenate(two, axis=1))
            for i in range(2):
                part = both[:, i * LANES : (i + 1) * LANES]
                spectrum[base + start + pair + i] = part[:LY] + swapped(part[LY:]) * flip
        return carry

    lax.fori_loop(0, field.shape[0] // PLANES, planes, 0)


def volume_kernel(odd, inside, own, near, far, z_wide, y_table, y_band, z_band, spectrum, norm, summed):
    count = own.shape[0]
    is_odd = odd[0] == 1
    low = jnp.where(is_odd, 0, 2 * count)
    scale = inside[0].astype(jnp.float32)
    transform(own, spectrum, count, None, z_wide, y_table)
    transform(near, spectrum, low, None, z_wide, y_table)
    transform(far, spectrum, 2 * count - low, scale, z_wide, y_table)

    for step in range(NY // 8):
        at = pl.ds(step * 8, 8)
        below, above = [], []
        for x in range(count):
            one, two = near[x, at, :], far[x, at, :] * scale
            below.append(jnp.where(is_odd, one, two))
            above.append(jnp.where(is_odd, two, one))
        level = [value * value for value in below + [own[x, at, :] for x in range(count)] + above]
        width = 1
        while width < TS:
            level = [level[x] + level[x + width] for x in range(len(level) - width)]
            width *= 2
        for x in range(count):
            summed[x, at, :] = level[x]

    parts = y_band.shape[0] // count
    along_y = []
    for x in range(count):
        high, low = split(summed[x])
        along_y.append(dot(y_band[...], jnp.concatenate([high, low], axis=0)))
    rows_of = y_band.shape[0] // parts
    total = None
    for part in range(parts):
        piece = [value[part * rows_of : (part + 1) * rows_of] for value in along_y]
        high, low = split(jnp.concatenate(piece, axis=0))
        table = lane_block(z_band[...], part, parts)
        term = dot(high, table) + dot(low, table)
        total = term if total is None else total + term
    norm[...] = 1.0 / (SCALE * jnp.sqrt(total * SCALE**-2 + TS**3 * 1e-06))


def slide(plane, taps, count):
    if count <= 2:
        return [functools.reduce(jnp.add, [plane[x + a] * tap for a, tap in enumerate(taps)]) for x in range(count)]
    half = count // 2
    need = half + len(taps) // 2 - 1
    even, odd = plane[0::2], plane[1::2]
    first, second = taps[0::2], taps[1::2]
    shared = slide(odd[:need], [one + two for one, two in zip(first, second)], half)
    low = slide([even[i] - odd[i] for i in range(need)], first, half)
    high = slide([even[i + 1] - odd[i] for i in range(need)], second, half)
    return [shared[x // 2] + (high if x % 2 else low)[x // 2] for x in range(count)]


def template_kernel(
    apart, held, four, eight, twelve, spectrum, norm, z_high, z_low, y_table, back_y, back_high, back_low, scores, same, cross, product
):
    flip = sign()
    first = flip > 0
    values = held[...].astype(jnp.float32)
    for step, other in ((4, four), (8, eight), (12, twelve)):
        values = jnp.where(apart[0] == step, other[...].astype(jnp.float32), values)
    size = values.shape[0] * values.shape[1]
    centred = values - jnp.sum(values) / size
    normed = centred / jnp.sqrt(jnp.sum(centred * centred) / size + 1e-06)
    groups = values.shape[1] // TS
    along_z = dot_right(normed, row_blocks(z_high[...], groups), row_blocks(z_low[...], groups))
    deep = TS // groups

    def tap(a):
        rows = along_z[a * deep : (a + 1) * deep]
        return jnp.concatenate([rows[:, j * LANES : (j + 1) * LANES] for j in range(groups)], axis=0)

    for a in range(0, TS, 2):
        both = dot_left(y_table[...], jnp.concatenate([tap(a), tap(a + 1)], axis=1))
        for i in range(2):
            part = both[:, i * LANES : (i + 1) * LANES]
            value = part[:LY] + swapped(part[LY:]) * flip
            turned = swapped(value)
            same[a + i] = jnp.where(first, value, turned)
            cross[a + i] = jnp.where(first, -turned, value)

    out = spectrum.shape[0] - TS

    def rows(step, carry):
        at = pl.ds(pl.multiple_of(step * 8, 8), 8)
        plane = [spectrum[x, at, :] for x in range(out + TS)]
        straight = slide(plane, [same[a, at, :] for a in range(TS)], out)
        for x in range(out):
            product[x, at, :] = straight[x]
        turned = slide(plane, [cross[a, at, :] for a in range(TS)], out)
        for x in range(out):
            product[x, at, :] = product[x, at, :] + swapped(turned[x])
        return carry

    lax.fori_loop(0, LY // 8, rows, 0)

    fields = []
    for x in range(0, out, 2):
        both = dot_left(back_y[...], jnp.concatenate([product[x], product[x + 1]], axis=1))
        for i in range(2):
            part = both[:, i * LANES : (i + 1) * LANES]
            fields.append(part[:NY] - swapped(part[NY:]) * flip)
    parts = back_high.shape[1] // NZ
    rows_of = NY // parts
    columns = [
        jnp.concatenate([value[j * rows_of : (j + 1) * rows_of] for value in fields], axis=0) for j in range(parts)
    ]
    result = dot_right(
        jnp.concatenate(columns, axis=1), lane_blocks(back_high[...], parts), lane_blocks(back_low[...], parts)
    ) * norm[...]
    for x in range(out):
        scores[:, x, :] = result[x * rows_of : (x + 1) * rows_of]


def cost(flops):
    return pl.CostEstimate(flops=flops, bytes_accessed=flops // 1000, transcendentals=0)


PARAMS = pltpu.CompilerParams(vmem_limit_bytes=24 * 2**20)
IN_VMEM = pl.BlockSpec(memory_space=pltpu.VMEM)
IN_SMEM = pl.BlockSpec(memory_space=pltpu.SMEM)


def volume_tables():
    return [wide_right(forward_z(HALF, NZ)), stacked_left(forward_y(np.arange(NY) + HALF))]


def volume_side(odd, inside, own, near, far, parts):
    count = own.shape[0]
    rows_of = NY // parts
    order = np.arange(NY).reshape(rows_of, parts).T.reshape(-1)
    y_band = band(NY).T[order].astype(jnp.bfloat16)
    tables = volume_tables() + [
        np.concatenate([y_band, y_band], axis=1),
        np.tile(band(NZ), (1, parts)).astype(jnp.bfloat16),
    ]
    return pl.pallas_call(
        volume_kernel,
        out_shape=(
            jax.ShapeDtypeStruct((3 * count, LY, LANES), jnp.float32),
            jax.ShapeDtypeStruct((count * rows_of, parts * NZ), jnp.float32),
        ),
        in_specs=[IN_SMEM, IN_SMEM] + [IN_VMEM] * 7,
        out_specs=(IN_VMEM, IN_VMEM),
        scratch_shapes=[pltpu.VMEM((count, NY, NZ), jnp.float32)],
        compiler_params=PARAMS,
        cost_estimate=cost(10**6),
        name="volume_side",
    )(odd, inside, own, near, far, *[jnp.asarray(table) for table in tables])


def template_side(apart, candidates, spectrum, norm, parts):
    out = spectrum.shape[0] - TS
    rows_of = NY // parts
    groups = LANES // TS
    order = np.arange(NY).reshape(rows_of, parts).T.reshape(-1)
    taps = np.arange(TS).reshape(TS // groups, groups).T.reshape(-1)
    tables = (
        *halves(np.tile(forward_z(0, TS), (groups, 1))),
        stacked_left(forward_y(taps)),
        stacked_left(inverse_y(order)),
        *halves(np.tile(inverse_z(), (1, parts))),
    )
    return pl.pallas_call(
        template_kernel,
        out_shape=jax.ShapeDtypeStruct((rows_of, out, parts * NZ), jnp.float32),
        in_specs=[IN_SMEM] + [IN_VMEM] * 12,
        out_specs=IN_VMEM,
        scratch_shapes=[
            pltpu.VMEM((TS, LY, LANES), jnp.float32),
            pltpu.VMEM((TS, LY, LANES), jnp.float32),
            pltpu.VMEM((out, LY, LANES), jnp.float32),
        ],
        compiler_params=PARAMS,
        cost_estimate=cost(3 * 10**9),
        name="template_side",
    )(apart, *candidates, spectrum, norm, *[jnp.asarray(table) for table in tables])


def join_kernel(scores, best, mass):
    top = scores[0]
    total = jnp.exp(sharpness * top)
    for index in range(1, scores.shape[0]):
        value = scores[index]
        top = jnp.maximum(top, value)
        total = total + jnp.exp(sharpness * value)
    best[...] = top
    mass[...] = jnp.log(total) / sharpness


def join(scores):
    shape = jax.ShapeDtypeStruct(scores.shape[1:], jnp.float32)
    return pl.pallas_call(
        join_kernel,
        out_shape=(shape, shape),
        in_specs=[IN_VMEM],
        out_specs=(IN_VMEM, IN_VMEM),
        compiler_params=PARAMS,
        name="join",
    )(scores)


def exchange(value, step):
    return lax.ppermute(value, "space", [(i, i ^ step) for i in range(lax.axis_size("space"))])


def next_slab(slab):
    count, copies = lax.axis_size("space"), lax.axis_size("rot")
    pairs = []
    for first in range(1, count, 2):
        ahead = ROT_X if first % 4 == 3 else 0
        for copy in range(copies):
            one = first * copies + copy
            two = (first + 1) % count * copies + (copy + ahead) % copies
            pairs += [(one, two), (two, one)]
    return lax.ppermute(slab, ("space", "rot"), pairs)


def shards(tomogram, templates, rot_ids):
    parts = lax.axis_size("rot")
    me = lax.axis_index("space")
    bank = templates.shape[0]
    wanted = rot_ids[0]
    apart = me ^ (wanted // bank)
    held = lax.dynamic_index_in_dim(templates, wanted % bank, 0, keepdims=False)
    scaled = tomogram * SCALE
    sent = scaled.astype(jnp.float16)
    held = jnp.where((apart & 1) == 0, held, exchange(held, 1))
    held, sent, scaled = lax.optimization_barrier((held, sent, scaled))
    near = exchange(scaled, 1).reshape(-1, NY, NZ)
    own = scaled.reshape(-1, NY, NZ)
    far = next_slab(sent)
    held = jnp.where((apart & 2) == 0, held, exchange(held, 2))
    held, near, own = lax.optimization_barrier((held, near, own))
    others = [exchange(held, step) for step in (4, 8, 12)]
    candidates = [value.reshape(-1, LANES) for value in (held, *others)]
    far = far.astype(jnp.float32).reshape(-1, NY, NZ)
    inside = ((me > 0) & (me < lax.axis_size("space") - 1)).astype(jnp.int32).reshape(1)
    spectrum, norm = volume_side((me & 1).reshape(1), inside, own, near, far, NY // parts)
    blocks = template_side((apart & 12).reshape(1), candidates, spectrum, norm, NY // parts)
    arrived = lax.all_to_all((blocks * SENT).astype(jnp.float16), "rot", 0, 0)
    return join(arrived.astype(jnp.float32) * (1.0 / SENT))


def solution(mesh):
    return jax.shard_map(
        shards,
        mesh=mesh,
        in_specs=(P("space", None), P("space", None), P("rot")),
        out_specs=(P("space", "rot"), P("space", "rot")),
        check_vma=False,
    )
```

```python
import functools
import math

import jax
import jax.numpy as jnp
import numpy as np
from jax import lax
from jax.experimental import pallas as pl
from jax.experimental.pallas import tpu as pltpu
from jax.sharding import PartitionSpec as P

NY = 64
NZ = 96
TS = 32
HALF = TS // 2
LY = NY + HALF
LZ = NZ + HALF
KZ = LZ // 2 + 1
LANES = 128
MID = LANES // 2

sharpness = 0.4
SENT = 256.0
SCALE = 8192.0
ROT_X = 4
SEND_ORDER = list(range(15, -1, -1))


def angles(length, rows, columns):
    return (np.outer(rows, columns) % length) * (2.0 * math.pi / length)


def halves(table):
    high = np.asarray(table, np.float32).astype(jnp.bfloat16)
    low = (np.asarray(table, np.float64) - high.astype(np.float64)).astype(jnp.bfloat16)
    return high, low


def forward_z(first, count):
    turn = angles(LZ, np.arange(count) + first, np.arange(KZ))
    table = np.zeros((count, LANES))
    table[:, :KZ] = np.cos(turn)
    table[:, MID : MID + KZ] = -np.sin(turn)
    return table


def forward_y(positions):
    turn = angles(LY, np.arange(LY), positions)
    return np.concatenate([np.cos(turn), np.sin(turn)], axis=0)


def inverse_y(order):
    turn = angles(LY, order, np.arange(LY))
    return np.concatenate([np.cos(turn), np.sin(turn)], axis=0)


def inverse_z():
    turn = angles(LZ, np.arange(KZ), np.arange(NZ))
    weight = np.where((np.arange(KZ) == 0) | (np.arange(KZ) == LZ // 2), 1.0, 2.0) / (LY * LZ)
    table = np.zeros((LANES, NZ))
    table[:KZ] = np.cos(turn) * weight[:, None]
    table[MID : MID + KZ] = -np.sin(turn) * weight[:, None]
    return table


def band(count):
    offset = np.arange(count)[:, None] + HALF - np.arange(count)[None, :]
    return ((offset >= 0) & (offset < TS)).astype(np.float64)


def stacked_left(table):
    high, low = halves(table)
    return np.concatenate([high, high, low], axis=1)


def wide_right(table):
    high, low = halves(table)
    rows = np.zeros((LANES - table.shape[0], 2 * table.shape[1]), high.dtype)
    first = np.concatenate([high, low], axis=1)
    second = np.concatenate([high, np.zeros_like(high)], axis=1)
    return np.concatenate([first, rows, second, rows], axis=0)


def split(values):
    high = values.astype(jnp.bfloat16)
    low = (values - high.astype(jnp.float32)).astype(jnp.bfloat16)
    return high, low


def dot(left, right):
    return jnp.dot(left, right, preferred_element_type=jnp.float32)


def dot_right(values, high_table, low_table):
    high, low = split(values)
    return dot(high, high_table) + dot(low, high_table) + dot(high, low_table)


def dot_wide(values, table):
    high, low = split(values)
    blank = [jnp.zeros((values.shape[0], LANES - values.shape[1]), jnp.bfloat16)] if values.shape[1] < LANES else []
    both = dot(jnp.concatenate([high, *blank, low, *blank], axis=1), table)
    return both[:, : both.shape[1] // 2] + both[:, both.shape[1] // 2 :]


def dot_left(stack, values):
    high, low = split(values)
    return dot(stack, jnp.concatenate([high, low, high], axis=0))


def lane_block(tile, part, parts):
    width = tile.shape[1] // parts
    lane = lax.broadcasted_iota(jnp.int32, (1, tile.shape[1]), 1)
    keep = (lane >= part * width) & (lane < (part + 1) * width)
    return tile * keep.astype(jnp.float32).astype(jnp.bfloat16)


def row_block(tile, part, parts):
    height = tile.shape[0] // parts
    row = lax.broadcasted_iota(jnp.int32, tile.shape, 0)
    keep = (row >= part * height) & (row < (part + 1) * height)
    return tile * keep.astype(jnp.float32).astype(jnp.bfloat16)


def row_blocks(tile, parts):
    return jnp.concatenate([row_block(tile, part, parts) for part in range(parts)], axis=1)


def sign():
    lane = lax.broadcasted_iota(jnp.int32, (1, LANES), 1)
    return jnp.where(lane < MID, 1.0, -1.0).astype(jnp.float32)


def swapped(values):
    return pltpu.roll(values, MID, 1)


PLANES = 16


def transform(field, spectrum, base, scale, z_wide, y_table):
    flip = sign()

    def planes(step, carry):
        start = step * PLANES
        block = field[pl.ds(start, PLANES)].reshape(PLANES * NY, NZ)
        along_z = dot_wide(block if scale is None else block * scale, z_wide[...])
        for pair in range(0, PLANES, 2):
            two = [along_z[(pair + i) * NY : (pair + i + 1) * NY] for i in range(2)]
            both = dot_left(y_table[...], jnp.concatenate(two, axis=1))
            for i in range(2):
                part = both[:, i * LANES : (i + 1) * LANES]
                spectrum[base + start + pair + i] = part[:LY] + swapped(part[LY:]) * flip
        return carry

    lax.fori_loop(0, field.shape[0] // PLANES, planes, 0)


def volume_kernel(odd, inside, own, near, far, z_wide, y_table, y_band, z_band, spectrum, norm, summed):
    count = own.shape[0]
    is_odd = odd[0] == 1
    low = jnp.where(is_odd, 0, 2 * count)
    scale = inside[0].astype(jnp.float32)
    transform(own, spectrum, count, None, z_wide, y_table)
    transform(near, spectrum, low, None, z_wide, y_table)
    transform(far, spectrum, 2 * count - low, scale, z_wide, y_table)

    for step in range(NY // 8):
        at = pl.ds(step * 8, 8)
        below, above = [], []
        for x in range(count):
            one, two = near[x, at, :], far[x, at, :] * scale
            below.append(jnp.where(is_odd, one, two))
            above.append(jnp.where(is_odd, two, one))
        level = [value * value for value in below + [own[x, at, :] for x in range(count)] + above]
        width = 1
        while width < TS:
            level = [level[x] + level[x + width] for x in range(len(level) - width)]
            width *= 2
        for x in range(count):
            summed[x, at, :] = level[x]

    parts = y_band.shape[0] // count
    along_y = []
    for x in range(count):
        high, low = split(summed[x])
        along_y.append(dot(y_band[...], jnp.concatenate([high, low], axis=0)))
    rows_of = y_band.shape[0] // parts
    total = None
    for part in range(parts):
        piece = [value[part * rows_of : (part + 1) * rows_of] for value in along_y]
        high, low = split(jnp.concatenate(piece, axis=0))
        table = lane_block(z_band[...], part, parts)
        term = dot(high, table) + dot(low, table)
        total = term if total is None else total + term
    norm[...] = 1.0 / (SCALE * jnp.sqrt(total * SCALE**-2 + TS**3 * 1e-06))


def slide(plane, taps, others, count):
    if count <= 2:
        return [
            [functools.reduce(jnp.add, [plane[x + a] * tap for a, tap in enumerate(row)]) for x in range(count)]
            for row in (taps, others)
        ]
    half = count // 2
    need = half + len(taps) // 2 - 1
    even, odd = plane[0::2], plane[1::2]
    first, second = [row[0::2] for row in (taps, others)], [row[1::2] for row in (taps, others)]
    added = [[one + two for one, two in zip(*pair)] for pair in zip(first, second)]
    shared = slide(odd[:need], *added, half)
    low = slide([even[i] - odd[i] for i in range(need)], *first, half)
    high = slide([even[i + 1] - odd[i] for i in range(need)], *second, half)
    return [[shared[r][x // 2] + (high if x % 2 else low)[r][x // 2] for x in range(count)] for r in range(2)]


def template_kernel(
    apart, held, four, eight, twelve, spectrum, norm, z_high, z_low, y_table, back_y, back_high, back_low, scores, same, cross, product
):
    flip = sign()
    first = flip > 0
    values = held[...].astype(jnp.float32)
    for step, other in ((4, four), (8, eight), (12, twelve)):
        values = jnp.where(apart[0] == step, other[...].astype(jnp.float32), values)
    size = values.shape[0] * values.shape[1]
    centred = values - jnp.sum(values) / size
    scale = 1.0 / jnp.sqrt(jnp.full((1, 1), jnp.sum(centred * centred) / size) + 1e-06)
    groups = values.shape[1] // TS
    along_z = dot_right(centred, row_blocks(z_high[...], groups), row_blocks(z_low[...], groups))
    deep = TS // groups

    def tap(a):
        rows = along_z[a * deep : (a + 1) * deep]
        return jnp.concatenate([rows[:, j * LANES : (j + 1) * LANES] for j in range(groups)], axis=0)

    for a in range(0, TS, 2):
        both = dot_left(y_table[...], jnp.concatenate([tap(a), tap(a + 1)], axis=1))
        for i in range(2):
            part = both[:, i * LANES : (i + 1) * LANES]
            value = part[:LY] + swapped(part[LY:]) * flip
            turned = swapped(value)
            same[a + i] = jnp.where(first, value, turned)
            cross[a + i] = jnp.where(first, -turned, value)

    out = spectrum.shape[0] - TS

    def rows(step, carry):
        at = pl.ds(pl.multiple_of(step * 8, 8), 8)
        plane = [spectrum[x, at, :] for x in range(out + TS)]
        taps, others = [[table[a, at, :] for a in range(TS)] for table in (same, cross)]
        straight, turned = slide(plane, taps, others, out)
        for x in range(out):
            product[x, at, :] = straight[x] + swapped(turned[x])
        return carry

    lax.fori_loop(0, LY // 8, rows, 0)

    fields = []
    for x in range(0, out, 2):
        both = dot_left(back_y[...], jnp.concatenate([product[x], product[x + 1]], axis=1))
        for i in range(2):
            part = both[:, i * LANES : (i + 1) * LANES]
            fields.append(part[:NY] - swapped(part[NY:]) * flip)
    parts = norm.shape[1] // NZ
    rows_of = NY // parts
    columns = [
        jnp.concatenate([value[j * rows_of : (j + 1) * rows_of] for value in fields], axis=0) for j in range(parts)
    ]
    result = jnp.concatenate([dot_right(column, back_high[...], back_low[...]) for column in columns], axis=1)
    result = result * (norm[...] * scale)
    for x in range(out):
        scores[:, x, :] = result[x * rows_of : (x + 1) * rows_of]


def cost(flops):
    return pl.CostEstimate(flops=flops, bytes_accessed=flops // 1000, transcendentals=0)


PARAMS = pltpu.CompilerParams(vmem_limit_bytes=24 * 2**20)
IN_VMEM = pl.BlockSpec(memory_space=pltpu.VMEM)
IN_SMEM = pl.BlockSpec(memory_space=pltpu.SMEM)


def volume_tables():
    return [wide_right(forward_z(HALF, NZ)), stacked_left(forward_y(np.arange(NY) + HALF))]


def volume_side(odd, inside, own, near, far, parts):
    count = own.shape[0]
    rows_of = NY // parts
    order = np.arange(NY).reshape(rows_of, parts)[SEND_ORDER].T.reshape(-1)
    y_band = band(NY).T[order].astype(jnp.bfloat16)
    tables = volume_tables() + [
        np.concatenate([y_band, y_band], axis=1),
        np.tile(band(NZ), (1, parts)).astype(jnp.bfloat16),
    ]
    return pl.pallas_call(
        volume_kernel,
        out_shape=(
            jax.ShapeDtypeStruct((3 * count, LY, LANES), jnp.float32),
            jax.ShapeDtypeStruct((count * rows_of, parts * NZ), jnp.float32),
        ),
        in_specs=[IN_SMEM, IN_SMEM] + [IN_VMEM] * 7,
        out_specs=(IN_VMEM, IN_VMEM),
        scratch_shapes=[pltpu.VMEM((count, NY, NZ), jnp.float32)],
        compiler_params=PARAMS,
        cost_estimate=cost(10**6),
        name="volume_side",
    )(odd, inside, own, near, far, *[jnp.asarray(table) for table in tables])


def template_side(apart, candidates, spectrum, norm, parts):
    out = spectrum.shape[0] - TS
    rows_of = NY // parts
    groups = LANES // TS
    order = np.arange(NY).reshape(rows_of, parts)[SEND_ORDER].T.reshape(-1)
    taps = np.arange(TS).reshape(TS // groups, groups).T.reshape(-1)
    tables = (
        *halves(np.tile(forward_z(0, TS), (groups, 1))),
        stacked_left(forward_y(taps)),
        stacked_left(inverse_y(order)),
        *halves(inverse_z()),
    )
    return pl.pallas_call(
        template_kernel,
        out_shape=jax.ShapeDtypeStruct((rows_of, out, parts * NZ), jnp.float32),
        in_specs=[IN_SMEM] + [IN_VMEM] * 12,
        out_specs=IN_VMEM,
        scratch_shapes=[
            pltpu.VMEM((TS, LY, LANES), jnp.float32),
            pltpu.VMEM((TS, LY, LANES), jnp.float32),
            pltpu.VMEM((out, LY, LANES), jnp.float32),
        ],
        compiler_params=PARAMS,
        cost_estimate=cost(3 * 10**9),
        name="template_side",
    )(apart, *candidates, spectrum, norm, *[jnp.asarray(table) for table in tables])


def join_kernel(scores, best, mass):
    top = scores[0]
    total = jnp.exp(sharpness * top)
    for index in range(1, scores.shape[0]):
        value = scores[index]
        top = jnp.maximum(top, value)
        total = total + jnp.exp(sharpness * value)
    best[...] = top
    mass[...] = jnp.log(total) / sharpness


def join(scores):
    shape = jax.ShapeDtypeStruct(scores.shape[1:], jnp.float32)
    return pl.pallas_call(
        join_kernel,
        out_shape=(shape, shape),
        in_specs=[IN_VMEM],
        out_specs=(IN_VMEM, IN_VMEM),
        compiler_params=PARAMS,
        name="join",
    )(scores)


def exchange(value, step):
    return lax.ppermute(value, "space", [(i, i ^ step) for i in range(lax.axis_size("space"))])


def next_slab(slab):
    count, copies = lax.axis_size("space"), lax.axis_size("rot")
    pairs = []
    for first in range(1, count, 2):
        ahead = ROT_X if first % 4 == 3 else 0
        for copy in range(copies):
            one = first * copies + copy
            two = (first + 1) % count * copies + (copy + ahead) % copies
            pairs += [(one, two), (two, one)]
    return lax.ppermute(slab, ("space", "rot"), pairs)


def shards(tomogram, templates, rot_ids):
    parts = lax.axis_size("rot")
    me = lax.axis_index("space")
    bank = templates.shape[0]
    wanted = rot_ids[0]
    apart = me ^ lax.div(wanted, bank)
    held = lax.dynamic_slice(templates, (lax.rem(wanted, bank), 0), (1, templates.shape[1])).reshape(-1)
    scaled = tomogram * SCALE
    sent = scaled.astype(jnp.float16)
    held = jnp.where((apart & 1) == 0, held, exchange(held, 1))
    held, sent, scaled = lax.optimization_barrier((held, sent, scaled))
    near = exchange(scaled, 1).reshape(-1, NY, NZ)
    own = scaled.reshape(-1, NY, NZ)
    far = next_slab(sent)
    held = jnp.where((apart & 2) == 0, held, exchange(held, 2))
    held, near, own = lax.optimization_barrier((held, near, own))
    others = [exchange(held, step) for step in (4, 8, 12)]
    candidates = [value.reshape(-1, LANES) for value in (held, *others)]
    far = far.astype(jnp.float32).reshape(-1, NY, NZ)
    inside = ((me > 0) & (me < lax.axis_size("space") - 1)).astype(jnp.int32).reshape(1)
    spectrum, norm = volume_side((me & 1).reshape(1), inside, own, near, far, NY // parts)
    blocks = template_side((apart & 12).reshape(1), candidates, spectrum, norm, NY // parts)
    arrived = lax.all_to_all((blocks * SENT).astype(jnp.float16), "rot", 0, 0, axis_index_groups=[SEND_ORDER])
    return join(arrived.astype(jnp.float32) * (1.0 / SENT))


def solution(mesh):
    return jax.shard_map(
        shards,
        mesh=mesh,
        in_specs=(P("space", None), P("space", None), P("rot")),
        out_specs=(P("space", "rot"), P("space", "rot")),
        check_vma=False,
    )
```

```python
import functools
import math

import jax
import jax.numpy as jnp
import numpy as np
from jax import lax
from jax.experimental import pallas as pl
from jax.experimental.pallas import tpu as pltpu
from jax.sharding import PartitionSpec as P

NY = 64
NZ = 96
TS = 32
HALF = TS // 2
LY = NY + HALF
LZ = NZ + HALF
KZ = LZ // 2 + 1
LANES = 128
MID = LANES // 2

sharpness = 0.4
SENT = 256.0
SCALE = 8192.0
ROT_X = 4
SEND_ORDER = list(range(15, -1, -1))


def angles(length, rows, columns):
    return (np.outer(rows, columns) % length) * (2.0 * math.pi / length)


def halves(table):
    high = np.asarray(table, np.float32).astype(jnp.bfloat16)
    low = (np.asarray(table, np.float64) - high.astype(np.float64)).astype(jnp.bfloat16)
    return high, low


def forward_z(first, count):
    turn = angles(LZ, np.arange(count) + first, np.arange(KZ))
    table = np.zeros((count, LANES))
    table[:, :KZ] = np.cos(turn)
    table[:, MID : MID + KZ] = -np.sin(turn)
    return table


def forward_y(positions):
    turn = angles(LY, np.arange(LY), positions)
    return np.concatenate([np.cos(turn), np.sin(turn)], axis=0)


def inverse_y(order):
    turn = angles(LY, order, np.arange(LY))
    return np.concatenate([np.cos(turn), np.sin(turn)], axis=0)


def inverse_z():
    turn = angles(LZ, np.arange(KZ), np.arange(NZ))
    weight = np.where((np.arange(KZ) == 0) | (np.arange(KZ) == LZ // 2), 1.0, 2.0) / (LY * LZ)
    table = np.zeros((LANES, NZ))
    table[:KZ] = np.cos(turn) * weight[:, None]
    table[MID : MID + KZ] = -np.sin(turn) * weight[:, None]
    return table


def band(count):
    offset = np.arange(count)[:, None] + HALF - np.arange(count)[None, :]
    return ((offset >= 0) & (offset < TS)).astype(np.float64)


def stacked_left(table):
    high, low = halves(table)
    return np.concatenate([high, high, low], axis=1)


def wide_right(table):
    high, low = halves(table)
    rows = np.zeros((LANES - table.shape[0], 2 * table.shape[1]), high.dtype)
    first = np.concatenate([high, low], axis=1)
    second = np.concatenate([high, np.zeros_like(high)], axis=1)
    return np.concatenate([first, rows, second, rows], axis=0)


def split(values):
    high = values.astype(jnp.bfloat16)
    low = (values - high.astype(jnp.float32)).astype(jnp.bfloat16)
    return high, low


def dot(left, right):
    return jnp.dot(left, right, preferred_element_type=jnp.float32)


def dot_right(values, high_table, low_table):
    high, low = split(values)
    return dot(high, high_table) + dot(low, high_table) + dot(high, low_table)


def dot_wide(values, table):
    high, low = split(values)
    blank = [jnp.zeros((values.shape[0], LANES - values.shape[1]), jnp.bfloat16)] if values.shape[1] < LANES else []
    both = dot(jnp.concatenate([high, *blank, low, *blank], axis=1), table)
    return both[:, : both.shape[1] // 2] + both[:, both.shape[1] // 2 :]


def dot_left(stack, values):
    high, low = split(values)
    return dot(stack, jnp.concatenate([high, low, high], axis=0))


def lane_block(tile, part, parts):
    width = tile.shape[1] // parts
    lane = lax.broadcasted_iota(jnp.int32, (1, tile.shape[1]), 1)
    keep = (lane >= part * width) & (lane < (part + 1) * width)
    return tile * keep.astype(jnp.float32).astype(jnp.bfloat16)


def row_block(tile, part, parts):
    height = tile.shape[0] // parts
    row = lax.broadcasted_iota(jnp.int32, tile.shape, 0)
    keep = (row >= part * height) & (row < (part + 1) * height)
    return tile * keep.astype(jnp.float32).astype(jnp.bfloat16)


def row_blocks(tile, parts):
    return jnp.concatenate([row_block(tile, part, parts) for part in range(parts)], axis=1)


def sign():
    lane = lax.broadcasted_iota(jnp.int32, (1, LANES), 1)
    return jnp.where(lane < MID, 1.0, -1.0).astype(jnp.float32)


def swapped(values):
    return pltpu.roll(values, MID, 1)


PLANES = 16


def transform(field, spectrum, base, scale, z_wide, y_table):
    flip = sign()

    def planes(step, carry):
        start = step * PLANES
        block = field[pl.ds(start, PLANES)].reshape(PLANES * NY, NZ)
        along_z = dot_wide(block if scale is None else block * scale, z_wide[...])
        for pair in range(0, PLANES, 2):
            two = [along_z[(pair + i) * NY : (pair + i + 1) * NY] for i in range(2)]
            both = dot_left(y_table[...], jnp.concatenate(two, axis=1))
            for i in range(2):
                part = both[:, i * LANES : (i + 1) * LANES]
                spectrum[base + start + pair + i] = part[:LY] + swapped(part[LY:]) * flip
        return carry

    lax.fori_loop(0, field.shape[0] // PLANES, planes, 0)


def volume_kernel(odd, inside, own, near, far, z_wide, y_table, y_band, z_band, spectrum, norm, summed):
    count = own.shape[0]
    is_odd = odd[0] == 1
    low = jnp.where(is_odd, 0, 2 * count)
    scale = inside[0].astype(jnp.float32)
    transform(own, spectrum, count, None, z_wide, y_table)
    transform(near, spectrum, low, None, z_wide, y_table)
    transform(far, spectrum, 2 * count - low, scale, z_wide, y_table)

    for step in range(NY // 8):
        at = pl.ds(step * 8, 8)
        below, above = [], []
        for x in range(count):
            one, two = near[x, at, :], far[x, at, :] * scale
            below.append(jnp.where(is_odd, one, two))
            above.append(jnp.where(is_odd, two, one))
        level = [value * value for value in below + [own[x, at, :] for x in range(count)] + above]
        width = 1
        while width < TS:
            level = [level[x] + level[x + width] for x in range(len(level) - width)]
            width *= 2
        for x in range(count):
            summed[x, at, :] = level[x]

    parts = y_band.shape[0] // count
    along_y = []
    for x in range(count):
        high, low = split(summed[x])
        along_y.append(dot(y_band[...], jnp.concatenate([high, low], axis=0)))
    rows_of = y_band.shape[0] // parts
    total = None
    for part in range(parts):
        piece = [value[part * rows_of : (part + 1) * rows_of] for value in along_y]
        high, low = split(jnp.concatenate(piece, axis=0))
        table = lane_block(z_band[...], part, parts)
        term = dot(high, table) + dot(low, table)
        total = term if total is None else total + term
    norm[...] = 1.0 / (SCALE * jnp.sqrt(total * SCALE**-2 + TS**3 * 1e-06))


def slide(plane, taps, others, count):
    if count <= 2:
        return [
            [functools.reduce(jnp.add, [plane[x + a] * tap for a, tap in enumerate(row)]) for x in range(count)]
            for row in (taps, others)
        ]
    half = count // 2
    need = half + len(taps) // 2 - 1
    even, odd = plane[0::2], plane[1::2]
    first, second = [row[0::2] for row in (taps, others)], [row[1::2] for row in (taps, others)]
    added = [[one + two for one, two in zip(*pair)] for pair in zip(first, second)]
    shared = slide(odd[:need], *added, half)
    low = slide([even[i] - odd[i] for i in range(need)], *first, half)
    high = slide([even[i + 1] - odd[i] for i in range(need)], *second, half)
    return [[shared[r][x // 2] + (high if x % 2 else low)[r][x // 2] for x in range(count)] for r in range(2)]


def template_kernel(
    apart, odd, held, four, eight, twelve, spectrum, norm, z_high, z_low, y_table, back_y, back_high, back_low, scores, same, cross, product
):
    flip = sign()
    first = flip > 0
    values = held[...].astype(jnp.float32)
    for step, other in ((4, four), (8, eight), (12, twelve)):
        values = jnp.where(apart[0] == step, other[...].astype(jnp.float32), values)
    size = values.shape[0] * values.shape[1]
    centred = values - jnp.sum(values) / size
    scale = 1.0 / jnp.sqrt(jnp.full((1, 1), jnp.sum(centred * centred) / size) + 1e-06)
    groups = values.shape[1] // TS
    along_z = dot_right(centred, row_blocks(z_high[...], groups), row_blocks(z_low[...], groups))
    deep = TS // groups

    def tap(a):
        rows = along_z[a * deep : (a + 1) * deep]
        return jnp.concatenate([rows[:, j * LANES : (j + 1) * LANES] for j in range(groups)], axis=0)

    for a in range(0, TS, 2):
        both = dot_left(y_table[...], jnp.concatenate([tap(a), tap(a + 1)], axis=1))
        for i in range(2):
            part = both[:, i * LANES : (i + 1) * LANES]
            value = part[:LY] + swapped(part[LY:]) * flip
            turned = swapped(value)
            same[a + i] = jnp.where(first, value, turned)
            cross[a + i] = jnp.where(first, -turned, value)

    out = spectrum.shape[0] - TS

    def rows(step, carry):
        at = pl.ds(pl.multiple_of(step * 8, 8), 8)
        plane = [spectrum[x, at, :] for x in range(out + TS)]
        taps, others = [[table[a, at, :] for a in range(TS)] for table in (same, cross)]
        straight, turned = slide(plane, taps, others, out)
        for x in range(out):
            product[x, at, :] = straight[x] + swapped(turned[x])
        return carry

    lax.fori_loop(0, LY // 8, rows, 0)

    fields = []
    for x in range(0, out, 2):
        both = dot_left(back_y[...], jnp.concatenate([product[x], product[x + 1]], axis=1))
        for i in range(2):
            part = both[:, i * LANES : (i + 1) * LANES]
            fields.append(part[:NY] - swapped(part[NY:]) * flip)
    parts = norm.shape[1] // NZ
    rows_of = NY // parts
    columns = [
        jnp.concatenate([value[j * rows_of : (j + 1) * rows_of] for value in fields], axis=0) for j in range(parts)
    ]
    result = jnp.concatenate([dot_right(column, back_high[...], back_low[...]) for column in columns], axis=1)
    result = result * (norm[...] * scale)
    for x in range(out):
        for quarter in range(4):
            part = rows_of // 4
            base = (quarter + (1 - 2 * (quarter % 2)) * odd[0]) * part
            scores[pl.ds(base, part), x, :] = result[x * rows_of + quarter * part : x * rows_of + (quarter + 1) * part]


def cost(flops):
    return pl.CostEstimate(flops=flops, bytes_accessed=flops // 1000, transcendentals=0)


PARAMS = pltpu.CompilerParams(vmem_limit_bytes=24 * 2**20)
IN_VMEM = pl.BlockSpec(memory_space=pltpu.VMEM)
IN_SMEM = pl.BlockSpec(memory_space=pltpu.SMEM)


def volume_tables():
    return [wide_right(forward_z(HALF, NZ)), stacked_left(forward_y(np.arange(NY) + HALF))]


def volume_side(odd, inside, own, near, far, parts):
    count = own.shape[0]
    rows_of = NY // parts
    order = np.arange(NY).reshape(rows_of, parts)[SEND_ORDER].T.reshape(-1)
    y_band = band(NY).T[order].astype(jnp.bfloat16)
    tables = volume_tables() + [
        np.concatenate([y_band, y_band], axis=1),
        np.tile(band(NZ), (1, parts)).astype(jnp.bfloat16),
    ]
    return pl.pallas_call(
        volume_kernel,
        out_shape=(
            jax.ShapeDtypeStruct((3 * count, LY, LANES), jnp.float32),
            jax.ShapeDtypeStruct((count * rows_of, parts * NZ), jnp.float32),
        ),
        in_specs=[IN_SMEM, IN_SMEM] + [IN_VMEM] * 7,
        out_specs=(IN_VMEM, IN_VMEM),
        scratch_shapes=[pltpu.VMEM((count, NY, NZ), jnp.float32)],
        compiler_params=PARAMS,
        cost_estimate=cost(10**6),
        name="volume_side",
    )(odd, inside, own, near, far, *[jnp.asarray(table) for table in tables])


def template_side(apart, odd, candidates, spectrum, norm, parts):
    out = spectrum.shape[0] - TS
    rows_of = NY // parts
    groups = LANES // TS
    order = np.arange(NY).reshape(rows_of, parts)[SEND_ORDER].T.reshape(-1)
    taps = np.arange(TS).reshape(TS // groups, groups).T.reshape(-1)
    tables = (
        *halves(np.tile(forward_z(0, TS), (groups, 1))),
        stacked_left(forward_y(taps)),
        stacked_left(inverse_y(order)),
        *halves(inverse_z()),
    )
    return pl.pallas_call(
        template_kernel,
        out_shape=jax.ShapeDtypeStruct((rows_of, out, parts * NZ), jnp.float32),
        in_specs=[IN_SMEM, IN_SMEM] + [IN_VMEM] * 12,
        out_specs=IN_VMEM,
        scratch_shapes=[
            pltpu.VMEM((TS, LY, LANES), jnp.float32),
            pltpu.VMEM((TS, LY, LANES), jnp.float32),
            pltpu.VMEM((out, LY, LANES), jnp.float32),
        ],
        compiler_params=PARAMS,
        cost_estimate=cost(3 * 10**9),
        name="template_side",
    )(apart, odd, *candidates, spectrum, norm, *[jnp.asarray(table) for table in tables])


def join_kernel(scores, best, mass):
    top = scores[0]
    total = jnp.exp(sharpness * top)
    for index in range(1, scores.shape[0]):
        value = scores[index]
        top = jnp.maximum(top, value)
        total = total + jnp.exp(sharpness * value)
    best[...] = top
    mass[...] = jnp.log(total) / sharpness


def join(scores):
    shape = jax.ShapeDtypeStruct(scores.shape[1:], jnp.float32)
    return pl.pallas_call(
        join_kernel,
        out_shape=(shape, shape),
        in_specs=[IN_VMEM],
        out_specs=(IN_VMEM, IN_VMEM),
        compiler_params=PARAMS,
        name="join",
    )(scores)


def exchange(value, step):
    return lax.ppermute(value, "space", [(i, i ^ step) for i in range(lax.axis_size("space"))])


def next_slab(slab):
    count, copies = lax.axis_size("space"), lax.axis_size("rot")
    pairs = []
    for first in range(1, count, 2):
        ahead = ROT_X if first % 4 == 3 else 0
        for copy in range(copies):
            one = first * copies + copy
            two = (first + 1) % count * copies + (copy + ahead) % copies
            pairs += [(one, two), (two, one)]
    return lax.ppermute(slab, ("space", "rot"), pairs)


def send_groups():
    size = len(SEND_ORDER) // 4
    groups = []
    for slab in range(lax.axis_size("space")):
        quarters = [SEND_ORDER[(place ^ (slab & 1)) * size :][:size] for place in range(4)]
        groups.append([slab * len(SEND_ORDER) + copy for quarter in quarters for copy in quarter])
    return groups


def shards(tomogram, templates, rot_ids):
    parts = lax.axis_size("rot")
    me = lax.axis_index("space")
    bank = templates.shape[0]
    wanted = rot_ids[0]
    apart = me ^ lax.div(wanted, bank)
    held = lax.dynamic_slice(templates, (lax.rem(wanted, bank), 0), (1, templates.shape[1])).reshape(-1)
    scaled = tomogram * SCALE
    sent = scaled.astype(jnp.float16)
    held = jnp.where((apart & 1) == 0, held, exchange(held, 1))
    held, sent, scaled = lax.optimization_barrier((held, sent, scaled))
    near = exchange(scaled, 1).reshape(-1, NY, NZ)
    own = scaled.reshape(-1, NY, NZ)
    far = next_slab(sent)
    held = jnp.where((apart & 2) == 0, held, exchange(held, 2))
    held, near, own = lax.optimization_barrier((held, near, own))
    others = [exchange(held, step) for step in (4, 8, 12)]
    candidates = [value.reshape(-1, LANES) for value in (held, *others)]
    far = far.astype(jnp.float32).reshape(-1, NY, NZ)
    inside = ((me > 0) & (me < lax.axis_size("space") - 1)).astype(jnp.int32).reshape(1)
    spectrum, norm = volume_side((me & 1).reshape(1), inside, own, near, far, NY // parts)
    blocks = template_side((apart & 12).reshape(1), (me & 1).reshape(1), candidates, spectrum, norm, NY // parts)
    arrived = lax.all_to_all((blocks * SENT).astype(jnp.float16), ("space", "rot"), 0, 0, axis_index_groups=send_groups())
    return join(arrived.astype(jnp.float32) * (1.0 / SENT))


def solution(mesh):
    return jax.shard_map(
        shards,
        mesh=mesh,
        in_specs=(P("space", None), P("space", None), P("rot")),
        out_specs=(P("space", "rot"), P("space", "rot")),
        check_vma=False,
    )
```

```python
import functools
import math

import jax
import jax.numpy as jnp
import numpy as np
from jax import lax
from jax.experimental import pallas as pl
from jax.experimental.pallas import tpu as pltpu
from jax.sharding import PartitionSpec as P

NY = 64
NZ = 96
TS = 32
HALF = TS // 2
LY = NY + HALF
LZ = NZ + HALF
KZ = LZ // 2 + 1
LANES = 128
MID = LANES // 2

sharpness = 0.4
SENT = 256.0
SCALE = 8192.0
ROT_X = 4
SEND_ORDER = list(range(15, -1, -1))


def angles(length, rows, columns):
    return (np.outer(rows, columns) % length) * (2.0 * math.pi / length)


def halves(table):
    high = np.asarray(table, np.float32).astype(jnp.bfloat16)
    low = (np.asarray(table, np.float64) - high.astype(np.float64)).astype(jnp.bfloat16)
    return high, low


def forward_z(first, count):
    turn = angles(LZ, np.arange(count) + first, np.arange(KZ))
    table = np.zeros((count, LANES))
    table[:, :KZ] = np.cos(turn)
    table[:, MID : MID + KZ] = -np.sin(turn)
    return table


def forward_y(positions):
    turn = angles(LY, np.arange(LY), positions)
    return np.concatenate([np.cos(turn), np.sin(turn)], axis=0)


def inverse_y(order):
    turn = angles(LY, order, np.arange(LY))
    return np.concatenate([np.cos(turn), np.sin(turn)], axis=0)


def inverse_z():
    turn = angles(LZ, np.arange(KZ), np.arange(NZ))
    weight = np.where((np.arange(KZ) == 0) | (np.arange(KZ) == LZ // 2), 1.0, 2.0) / (LY * LZ)
    table = np.zeros((LANES, NZ))
    table[:KZ] = np.cos(turn) * weight[:, None]
    table[MID : MID + KZ] = -np.sin(turn) * weight[:, None]
    return table


def band(count):
    offset = np.arange(count)[:, None] + HALF - np.arange(count)[None, :]
    return ((offset >= 0) & (offset < TS)).astype(np.float64)


def stacked_left(table):
    high, low = halves(table)
    return np.concatenate([high, high, low], axis=1)


def wide_right(table):
    high, low = halves(table)
    rows = np.zeros((LANES - table.shape[0], 2 * table.shape[1]), high.dtype)
    first = np.concatenate([high, low], axis=1)
    second = np.concatenate([high, np.zeros_like(high)], axis=1)
    return np.concatenate([first, rows, second, rows], axis=0)


def split(values):
    high = values.astype(jnp.bfloat16)
    low = (values - high.astype(jnp.float32)).astype(jnp.bfloat16)
    return high, low


def dot(left, right):
    return jnp.dot(left, right, preferred_element_type=jnp.float32)


def dot_right(values, high_table, low_table):
    high, low = split(values)
    return dot(high, high_table) + dot(low, high_table) + dot(high, low_table)


def dot_wide(values, table):
    high, low = split(values)
    blank = [jnp.zeros((values.shape[0], LANES - values.shape[1]), jnp.bfloat16)] if values.shape[1] < LANES else []
    both = dot(jnp.concatenate([high, *blank, low, *blank], axis=1), table)
    return both[:, : both.shape[1] // 2] + both[:, both.shape[1] // 2 :]


def dot_left(stack, values):
    high, low = split(values)
    return dot(stack, jnp.concatenate([high, low, high], axis=0))


def lane_block(tile, part, parts):
    width = tile.shape[1] // parts
    lane = lax.broadcasted_iota(jnp.int32, (1, tile.shape[1]), 1)
    keep = (lane >= part * width) & (lane < (part + 1) * width)
    return tile * keep.astype(jnp.float32).astype(jnp.bfloat16)


def row_block(tile, part, parts):
    height = tile.shape[0] // parts
    row = lax.broadcasted_iota(jnp.int32, tile.shape, 0)
    keep = (row >= part * height) & (row < (part + 1) * height)
    return tile * keep.astype(jnp.float32).astype(jnp.bfloat16)


def row_blocks(tile, parts):
    return jnp.concatenate([row_block(tile, part, parts) for part in range(parts)], axis=1)


def sign():
    lane = lax.broadcasted_iota(jnp.int32, (1, LANES), 1)
    return jnp.where(lane < MID, 1.0, -1.0).astype(jnp.float32)


def swapped(values):
    return pltpu.roll(values, MID, 1)


PLANES = 16


def transform(field, spectrum, base, scale, z_wide, y_table):
    flip = sign()

    def planes(step, carry):
        start = step * PLANES
        block = field[pl.ds(start, PLANES)].reshape(PLANES * NY, NZ)
        along_z = dot_wide(block if scale is None else block * scale, z_wide[...])
        for pair in range(0, PLANES, 2):
            two = [along_z[(pair + i) * NY : (pair + i + 1) * NY] for i in range(2)]
            both = dot_left(y_table[...], jnp.concatenate(two, axis=1))
            for i in range(2):
                part = both[:, i * LANES : (i + 1) * LANES]
                spectrum[base + start + pair + i] = part[:LY] + swapped(part[LY:]) * flip
        return carry

    lax.fori_loop(0, field.shape[0] // PLANES, planes, 0)


def volume_kernel(odd, inside, own, near, far, z_wide, y_table, y_band, z_band, spectrum, norm, summed):
    count = own.shape[0]
    is_odd = odd[0] == 1
    low = jnp.where(is_odd, 0, 2 * count)
    scale = inside[0].astype(jnp.float32)
    transform(own, spectrum, count, None, z_wide, y_table)
    transform(near, spectrum, low, None, z_wide, y_table)
    transform(far, spectrum, 2 * count - low, scale, z_wide, y_table)

    for step in range(NY // 8):
        at = pl.ds(step * 8, 8)
        below, above = [], []
        for x in range(count):
            one, two = near[x, at, :], far[x, at, :] * scale
            below.append(jnp.where(is_odd, one, two))
            above.append(jnp.where(is_odd, two, one))
        level = [value * value for value in below + [own[x, at, :] for x in range(count)] + above]
        width = 1
        while width < TS:
            level = [level[x] + level[x + width] for x in range(len(level) - width)]
            width *= 2
        for x in range(count):
            summed[x, at, :] = level[x]

    parts = y_band.shape[0] // count
    along_y = []
    for x in range(count):
        high, low = split(summed[x])
        along_y.append(dot(y_band[...], jnp.concatenate([high, low], axis=0)))
    rows_of = y_band.shape[0] // parts
    total = None
    for part in range(parts):
        piece = [value[part * rows_of : (part + 1) * rows_of] for value in along_y]
        high, low = split(jnp.concatenate(piece, axis=0))
        table = lane_block(z_band[...], part, parts)
        term = dot(high, table) + dot(low, table)
        total = term if total is None else total + term
    norm[...] = 1.0 / (SCALE * jnp.sqrt(total * SCALE**-2 + TS**3 * 1e-06))


def slide(plane, taps, others, count):
    if count <= 2:
        return [
            [functools.reduce(jnp.add, [plane[x + a] * tap for a, tap in enumerate(row)]) for x in range(count)]
            for row in (taps, others)
        ]
    half = count // 2
    need = half + len(taps) // 2 - 1
    even, odd = plane[0::2], plane[1::2]
    first, second = [row[0::2] for row in (taps, others)], [row[1::2] for row in (taps, others)]
    added = [[one + two for one, two in zip(*pair)] for pair in zip(first, second)]
    shared = slide(odd[:need], *added, half)
    low = slide([even[i] - odd[i] for i in range(need)], *first, half)
    high = slide([even[i + 1] - odd[i] for i in range(need)], *second, half)
    return [[shared[r][x // 2] + (high if x % 2 else low)[r][x // 2] for x in range(count)] for r in range(2)]


def template_kernel(
    apart, odd, held, four, eight, twelve, spectrum, norm, z_high, z_low, y_table, back_y, back_high, back_low, scores, same, cross, product
):
    flip = sign()
    first = flip > 0
    values = held[...].astype(jnp.float32)
    for step, other in ((4, four), (8, eight), (12, twelve)):
        values = jnp.where(apart[0] == step, other[...].astype(jnp.float32), values)
    size = values.shape[0] * values.shape[1]
    centred = values - jnp.sum(values) / size
    scale = 1.0 / jnp.sqrt(jnp.full((1, 1), jnp.sum(centred * centred) / size) + 1e-06)
    groups = values.shape[1] // TS
    along_z = dot_right(centred, row_blocks(z_high[...], groups), row_blocks(z_low[...], groups))
    deep = TS // groups

    def tap(a):
        rows = along_z[a * deep : (a + 1) * deep]
        return jnp.concatenate([rows[:, j * LANES : (j + 1) * LANES] for j in range(groups)], axis=0)

    for a in range(0, TS, 2):
        both = dot_left(y_table[...], jnp.concatenate([tap(a), tap(a + 1)], axis=1))
        for i in range(2):
            part = both[:, i * LANES : (i + 1) * LANES]
            value = part[:LY] + swapped(part[LY:]) * flip
            turned = swapped(value)
            same[a + i] = jnp.where(first, value, turned)
            cross[a + i] = jnp.where(first, -turned, value)

    out = spectrum.shape[0] - TS

    def rows(step, carry):
        at = pl.ds(pl.multiple_of(step * 8, 8), 8)
        plane = [spectrum[x, at, :] for x in range(out + TS)]
        taps, others = [[table[a, at, :] for a in range(TS)] for table in (same, cross)]
        straight, turned = slide(plane, taps, others, out)
        for x in range(out):
            product[x, at, :] = straight[x] + swapped(turned[x])
        return carry

    lax.fori_loop(0, LY // 8, rows, 0)

    fields = []
    for x in range(0, out, 2):
        both = dot_left(back_y[...], jnp.concatenate([product[x], product[x + 1]], axis=1))
        for i in range(2):
            part = both[:, i * LANES : (i + 1) * LANES]
            fields.append(part[:NY] - swapped(part[NY:]) * flip)
    parts = norm.shape[1] // NZ
    rows_of = NY // parts
    columns = [
        jnp.concatenate([value[j * rows_of : (j + 1) * rows_of] for value in fields], axis=0) for j in range(parts)
    ]
    result = jnp.concatenate([dot_right(column, back_high[...], back_low[...]) for column in columns], axis=1)
    result = result * (norm[...] * scale)
    for x in range(out):
        for quarter in range(4):
            part = rows_of // 4
            base = (quarter + (1 - 2 * (quarter % 2)) * odd[0]) * part
            scores[pl.ds(base, part), x, :] = result[x * rows_of + quarter * part : x * rows_of + (quarter + 1) * part]


def cost(flops):
    return pl.CostEstimate(flops=flops, bytes_accessed=flops // 1000, transcendentals=0)


PARAMS = pltpu.CompilerParams(vmem_limit_bytes=24 * 2**20)
IN_VMEM = pl.BlockSpec(memory_space=pltpu.VMEM)
IN_SMEM = pl.BlockSpec(memory_space=pltpu.SMEM)


def volume_tables():
    return [wide_right(forward_z(HALF, NZ)), stacked_left(forward_y(np.arange(NY) + HALF))]


def volume_side(odd, inside, own, near, far, parts):
    count = own.shape[0]
    rows_of = NY // parts
    order = np.arange(NY).reshape(rows_of, parts)[SEND_ORDER].T.reshape(-1)
    y_band = band(NY).T[order].astype(jnp.bfloat16)
    tables = volume_tables() + [
        np.concatenate([y_band, y_band], axis=1),
        np.tile(band(NZ), (1, parts)).astype(jnp.bfloat16),
    ]
    return pl.pallas_call(
        volume_kernel,
        out_shape=(
            jax.ShapeDtypeStruct((3 * count, LY, LANES), jnp.float32),
            jax.ShapeDtypeStruct((count * rows_of, parts * NZ), jnp.float32),
        ),
        in_specs=[IN_SMEM, IN_SMEM] + [IN_VMEM] * 7,
        out_specs=(IN_VMEM, IN_VMEM),
        scratch_shapes=[pltpu.VMEM((count, NY, NZ), jnp.float32)],
        compiler_params=PARAMS,
        cost_estimate=cost(10**6),
        name="volume_side",
    )(odd, inside, own, near, far, *[jnp.asarray(table) for table in tables])


def template_side(apart, odd, candidates, spectrum, norm, parts):
    out = spectrum.shape[0] - TS
    rows_of = NY // parts
    groups = LANES // TS
    order = np.arange(NY).reshape(rows_of, parts)[SEND_ORDER].T.reshape(-1)
    taps = np.arange(TS).reshape(TS // groups, groups).T.reshape(-1)
    tables = (
        *halves(np.tile(forward_z(0, TS), (groups, 1))),
        stacked_left(forward_y(taps)),
        stacked_left(inverse_y(order)),
        *halves(inverse_z()),
    )
    return pl.pallas_call(
        template_kernel,
        out_shape=jax.ShapeDtypeStruct((rows_of, out, parts * NZ), jnp.float32),
        in_specs=[IN_SMEM, IN_SMEM] + [IN_VMEM] * 12,
        out_specs=IN_VMEM,
        scratch_shapes=[
            pltpu.VMEM((TS, LY, LANES), jnp.float32),
            pltpu.VMEM((TS, LY, LANES), jnp.float32),
            pltpu.VMEM((out, LY, LANES), jnp.float32),
        ],
        compiler_params=PARAMS,
        cost_estimate=cost(3 * 10**9),
        name="template_side",
    )(apart, odd, *candidates, spectrum, norm, *[jnp.asarray(table) for table in tables])


def join_kernel(scores, best, mass):
    top = scores[0]
    total = jnp.exp(sharpness * top)
    for index in range(1, scores.shape[0]):
        value = scores[index]
        top = jnp.maximum(top, value)
        total = total + jnp.exp(sharpness * value)
    best[...] = top
    mass[...] = jnp.log(total) / sharpness


def join(scores):
    shape = jax.ShapeDtypeStruct(scores.shape[1:], jnp.float32)
    return pl.pallas_call(
        join_kernel,
        out_shape=(shape, shape),
        in_specs=[IN_VMEM],
        out_specs=(IN_VMEM, IN_VMEM),
        compiler_params=PARAMS,
        name="join",
    )(scores)


def exchange(value, step):
    return lax.ppermute(value, "space", [(i, i ^ step) for i in range(lax.axis_size("space"))])


def next_slab(slab):
    count, copies = lax.axis_size("space"), lax.axis_size("rot")
    pairs = []
    for first in range(1, count, 2):
        ahead = ROT_X if first % 4 == 3 else 0
        for copy in range(copies):
            one = first * copies + copy
            two = (first + 1) % count * copies + (copy + ahead) % copies
            pairs += [(one, two), (two, one)]
    return lax.ppermute(slab, ("space", "rot"), pairs)


def send_groups():
    size = len(SEND_ORDER) // 4
    groups = []
    for slab in range(lax.axis_size("space")):
        quarters = [SEND_ORDER[(place ^ (slab & 1)) * size :][:size] for place in range(4)]
        groups.append([slab * len(SEND_ORDER) + copy for quarter in quarters for copy in quarter])
    return groups


def shards(tomogram, templates, rot_ids):
    parts = lax.axis_size("rot")
    me = lax.axis_index("space")
    bank = templates.shape[0]
    wanted = rot_ids[0]
    apart = me ^ lax.div(wanted, bank)
    held = lax.dynamic_slice(templates, (lax.rem(wanted, bank), 0), (1, templates.shape[1])).reshape(-1)
    scaled = tomogram * SCALE
    sent = scaled.astype(jnp.float16)
    held = jnp.where((apart & 1) == 0, held, exchange(held, 1))
    held, sent, scaled = lax.optimization_barrier((held, sent, scaled))
    near = exchange(scaled, 1)
    own = scaled.reshape(-1, NY, NZ)
    far = next_slab(sent)
    held = jnp.where((apart & 2) == 0, held, exchange(held, 2))
    held, near, own = lax.optimization_barrier((held, near, own))
    others = [exchange(held, step) for step in (4, 8, 12)]
    candidates = [value.reshape(-1, LANES) for value in (held, *others)]
    far = far.astype(jnp.float32).reshape(-1, NY, NZ)
    near = near.reshape(-1, NY, NZ)
    inside = ((me > 0) & (me < lax.axis_size("space") - 1)).astype(jnp.int32).reshape(1)
    spectrum, norm = volume_side((me & 1).reshape(1), inside, own, near, far, NY // parts)
    blocks = template_side((apart & 12).reshape(1), (me & 1).reshape(1), candidates, spectrum, norm, NY // parts)
    arrived = lax.all_to_all((blocks * SENT).astype(jnp.float16), ("space", "rot"), 0, 0, axis_index_groups=send_groups())
    return join(arrived.astype(jnp.float32) * (1.0 / SENT))


def solution(mesh):
    return jax.shard_map(
        shards,
        mesh=mesh,
        in_specs=(P("space", None), P("space", None), P("rot")),
        out_specs=(P("space", "rot"), P("space", "rot")),
        check_vma=False,
    )
```
